128 devices in a mesh: leaf: 16 (over z, x_lo, core), head: 8 (over x_hi, y).
Axes of the slice: x: 4 (x_hi: 2, x_lo: 2; x = x_hi * 2 + x_lo), y: 4, z: 4, core: 2. Of those that a mesh axis runs over, the one named last changes fastest.
Arguments:
- query_rows: bfloat16 [12288, 4096], P('leaf', 'head')
- key_rows: bfloat16 [12288, 256], P('leaf')
- value_rows: bfloat16 [12288, 256], P('leaf'), may hold values from -6 to 6
- out_weight: bfloat16 [4096, 4096], P('head'), may hold values from -0.09375 to 0.09375
- out_grad: bfloat16 [12288, 4096], P(('leaf', 'head')), may hold values from -6 to 6
- seg_owner: int32 [42], replicated, may hold values from 0 to 15, as said below
- seg_parent: int32 [42], replicated, may hold values from -1 to 25, as said below
- seg_offset: int32 [42], replicated, may hold values from 0 to 640, as said below
- seg_length: int32 [42], replicated, may hold values from 1 to 512, as said below
Outputs:
- layer_out: bfloat16 [12288, 4096], P(('leaf', 'head'))
- query_grads: bfloat16 [12288, 4096], P('leaf', 'head')
- key_grads: bfloat16 [12288, 256], P(('leaf', 'head'))
- value_grads: bfloat16 [12288, 256], P(('leaf', 'head'))
- weight_grad: bfloat16 [4096, 4096], P('head', 'leaf')
The draws below stay inside these ranges and needn't reach their ends.
Inputs may be any that keep to these rules, and one draw needn't show every extreme that they name: seg_owner[i] is the leaf device of segment i; each device holds 2 leaves and at most one prompt or branch, never more than 768 live slots, and some device has all 768 slots live. `seg_parent`: segment 21 t is tree t's prompt (parent -1); 21 t + 1 to 21 t + 4 are its branches (parent 21 t); 21 t + 5 to 21 t + 20 are its leaves, four under each branch. Segment i fills slots seg_offset[i] to seg_offset[i] + seg_length[i] - 1 of its device, and no slot has two segments; every offset is a multiple of 128; a leaf's offset is at most 640, a branch's at most 512, a prompt's at most 256, and in every draw some leaf, some branch and some prompt sit at these latest offsets. `seg_length`: prompts have 512 tokens, branches 256, leaves at most 128, and one leaf of each tree exactly 128.
All inputs are finite; a program needn't handle non-finite values.
Results may differ from the reference program's by a relative error of at most 0.025.
Values may be sent and summed in bfloat16 or wider, within the bound.
No kernel may reach another device: no remote copies, remote signals or barrier semaphores. Data moves between devices by JAX's collectives and lax.ppermute only.
A program may use at most 192 MiB of HBM per device.

```python
import jax
import jax.numpy as jnp
from jax import lax

D = 4096
HEADS = 32
KV_HEADS = 2
HD = 128
GROUP = 16
LEAF_LEN = 128
BRANCH_LEN = 256
PROMPT_LEN = 512
LEAVES_DEV = 2
TREES = 2
ROWS_DEV = 768
SLOTS = 12288
N_LEAF = 16


def layout(key):
    key_leaf, key_dev, key_par, key_len, key_full, key_start, key_rank = jax.random.split(key, 7)
    leaf_perm = jax.random.permutation(key_leaf, TREES * 16).reshape(TREES, 16).astype(jnp.int32)
    dev_perm = jax.random.permutation(key_dev, N_LEAF).astype(jnp.int32)
    prompt_dev = dev_perm[:TREES].reshape(TREES, 1)
    branch_dev = dev_perm[TREES:5 * TREES].reshape(TREES, 4)
    leaf_dev = leaf_perm // LEAVES_DEV
    owner = jnp.concatenate([prompt_dev, branch_dev, leaf_dev], 1)
    windows = ROWS_DEV // LEAF_LEN
    prompt_start = jax.random.randint(key_start, (TREES,), 0, 3).astype(jnp.int32).at[0].set(2)
    branch_start = jax.random.randint(jax.random.fold_in(key_start, 1), (TREES, 4), 0, 5).astype(jnp.int32).at[0, 0].set(4)
    device_start = jnp.zeros((N_LEAF,), jnp.int32).at[prompt_dev.reshape(-1)].set(prompt_start).at[branch_dev.reshape(-1)].set(branch_start.reshape(-1))
    device_span = jnp.zeros((N_LEAF,), jnp.int32).at[prompt_dev.reshape(-1)].set(4).at[branch_dev.reshape(-1)].set(2)
    window_index = jnp.arange(windows, dtype=jnp.int32)[None, :]
    busy = (window_index >= device_start[:, None]) & (window_index < (device_start + device_span)[:, None])
    ranks = jax.vmap(lambda sub: jax.random.permutation(sub, windows))(jax.random.split(key_rank, N_LEAF)).astype(jnp.int32)
    forced_dev = dev_perm[5 * TREES]
    forced = (jnp.arange(N_LEAF, dtype=jnp.int32)[:, None] == forced_dev) & (window_index == windows - 1)
    ranks = jnp.where(forced, -1, ranks)
    scores = jnp.where(busy, 100, ranks)
    chosen = jnp.argsort(scores, axis=1, stable=True)[:, :LEAVES_DEV].astype(jnp.int32)
    leaf_window = chosen[leaf_dev, leaf_perm % LEAVES_DEV]
    offset = jnp.concatenate([device_start[prompt_dev] * LEAF_LEN, device_start[branch_dev] * LEAF_LEN, leaf_window * LEAF_LEN], 1).astype(jnp.int32)
    picks = jax.vmap(lambda sub: jax.random.permutation(sub, 16))(jax.random.split(key_par, TREES)).astype(jnp.int32)
    base = (jnp.arange(TREES, dtype=jnp.int32) * 21)[:, None]
    parent = jnp.concatenate([jnp.full((TREES, 1), -1, jnp.int32), jnp.broadcast_to(base, (TREES, 4)), base + 1 + picks // 4], 1)
    leaf_len = jax.random.randint(key_len, (TREES, 16), 1, LEAF_LEN + 1).astype(jnp.int32)
    full_pick = jax.random.randint(key_full, (TREES, 1), 0, 16)
    filled = (jnp.arange(16)[None, :] == full_pick) | (leaf_dev == dev_perm[0])
    leaf_len = jnp.where(filled, LEAF_LEN, leaf_len).astype(jnp.int32)
    length = jnp.concatenate([jnp.full((TREES, 1), PROMPT_LEN, jnp.int32), jnp.full((TREES, 4), BRANCH_LEN, jnp.int32), leaf_len], 1)
    return (owner.reshape(-1), parent.reshape(-1), offset.reshape(-1), length.reshape(-1))


def draw_seg_owner(key, part):
    owner, parent, offset, length = layout(key)
    return owner.astype(jnp.int32)


def draw_seg_parent(key, part):
    owner, parent, offset, length = layout(key)
    return parent.astype(jnp.int32)


def draw_seg_offset(key, part):
    owner, parent, offset, length = layout(key)
    return offset.astype(jnp.int32)


def draw_seg_length(key, part):
    owner, parent, offset, length = layout(key)
    return length.astype(jnp.int32)


def draw_query_rows(key, part):
    key = jax.random.fold_in(key, 11)
    base = jax.random.normal(key, (SLOTS, HEADS, HD), jnp.float32)
    return base.reshape(SLOTS, HEADS * HD).astype(jnp.bfloat16)


def draw_key_rows(key, part):
    key = jax.random.fold_in(key, 23)
    base = jax.random.normal(key, (SLOTS, KV_HEADS, HD), jnp.float32)
    return base.reshape(SLOTS, KV_HEADS * HD).astype(jnp.bfloat16)


def level_of(stream_key, dims, pieces, smallest, top_value):
    def one(axis_at, shards_of):
        draws = jax.random.uniform(jax.random.fold_in(jax.random.fold_in(stream_key, 6), axis_at), (shards_of,), jnp.float32, smallest / len(pieces), top_value / len(pieces))
        return jnp.repeat(jnp.exp(draws), dims[axis_at] // shards_of).reshape((-1,) + (1,) * (len(dims) - axis_at - 1))

    gain = one(*pieces[0])
    for cut in pieces[1:]:
        gain = gain * one(*cut)
    return gain


def centred(key, dims, spread, most, pieces=(), kind=jnp.bfloat16):
    drawn = spread * jax.random.normal(key, dims, jnp.float32)
    if pieces:
        drawn = drawn * level_of(key, dims, pieces, -0.22, 0.18)
    return jnp.clip(drawn, -most, most).astype(kind)


def setup_inputs(seed: int = 0) -> dict:
    seeds = jax.random.split(jax.random.key(seed), 10)
    return {
        "query_rows": draw_query_rows(jax.random.fold_in(seeds[9], 71), 0),
        "key_rows": draw_key_rows(jax.random.fold_in(seeds[9], 71), 0),
        "value_rows": centred(seeds[2], (SLOTS, KV_HEADS * HD), 1.0, 6.0, ((0, 16),)),
        "out_weight": centred(seeds[3], (HEADS * HD, D), (HEADS * HD) ** -0.5, 0.09375, ((0, 8),)),
        "out_grad": centred(seeds[4], (SLOTS, D), 1.0, 6.0, ((0, 128),)),
        "seg_owner": draw_seg_owner(jax.random.fold_in(seeds[9], 71), 0),
        "seg_parent": draw_seg_parent(jax.random.fold_in(seeds[9], 71), 0),
        "seg_offset": draw_seg_offset(jax.random.fold_in(seeds[9], 71), 0),
        "seg_length": draw_seg_length(jax.random.fold_in(seeds[9], 71), 0),
    }


NEG = -1e30


def segment_math(query_part, key_part, value_part, grad_part, allowed):
    scale = HD ** -0.5
    count_q = query_part.shape[0]
    query_f = query_part.astype(jnp.float32).reshape(count_q, KV_HEADS, GROUP, HD)
    key_f = key_part.astype(jnp.float32).reshape(-1, KV_HEADS, HD)
    value_f = value_part.astype(jnp.float32).reshape(-1, KV_HEADS, HD)
    grad_f = grad_part.astype(jnp.float32).reshape(count_q, KV_HEADS, GROUP, HD)
    mask = allowed[None, None]
    scores = jnp.einsum("qgjd,kgd->gjqk", query_f, key_f) * scale
    scores = jnp.where(mask, scores, NEG)
    row_top = jnp.max(scores, axis=3, keepdims=True)
    weights = jnp.exp(scores - row_top) * mask
    live = jnp.any(allowed, axis=1).astype(jnp.float32)
    row_total = jnp.sum(weights, axis=3, keepdims=True) + (1.0 - live)[None, None, :, None]
    probs_f = weights / row_total
    probs = lax.optimization_barrier(probs_f.astype(jnp.bfloat16)).astype(jnp.float32)
    attn = jnp.einsum("gjqk,kgd->qgjd", probs, value_f).astype(jnp.bfloat16)
    attn_f = lax.optimization_barrier(attn).astype(jnp.float32)
    delta = jnp.transpose(jnp.sum(grad_f * attn_f, axis=3), (1, 2, 0))
    dprobs = jnp.einsum("qgjd,kgd->gjqk", grad_f, value_f)
    dscores = (probs_f * (dprobs - delta[..., None]) * scale).astype(jnp.bfloat16)
    dscores_f = lax.optimization_barrier(dscores).astype(jnp.float32)
    query_grad = jnp.einsum("gjqk,kgd->qgjd", dscores_f, key_f).astype(jnp.bfloat16)
    key_grad = jnp.einsum("gjqk,qgjd->kgd", dscores_f, query_f)
    value_grad = jnp.einsum("gjqk,qgjd->kgd", probs, grad_f)
    return (attn.reshape(count_q, -1), query_grad.reshape(count_q, -1),
            key_grad.reshape(-1, KV_HEADS * HD), value_grad.reshape(-1, KV_HEADS * HD))


def add_rows(target, rows_value, first):
    count = rows_value.shape[0]
    old = lax.dynamic_slice_in_dim(target, first, count, 0)
    return lax.dynamic_update_slice_in_dim(target, old + rows_value, first, 0)


def level_pass(state, indices, depth, arrays):
    query_rows, key_rows, value_rows, attn_grad, seg_owner, seg_parent, seg_offset, seg_length = arrays
    caps = [PROMPT_LEN, BRANCH_LEN, LEAF_LEN]
    own_cap = caps[depth]
    elder = sum(caps[:depth])

    def one(state, index):
        chain = [index]
        for level in range(depth):
            chain.append(seg_parent[chain[-1]])
        chain = chain[::-1]
        starts = [(seg_owner[entry] * ROWS_DEV + seg_offset[entry]).astype(jnp.int32) for entry in chain]
        key_part = jnp.concatenate([lax.dynamic_slice_in_dim(key_rows, starts[level], caps[level], 0) for level in range(depth + 1)], 0)
        value_part = jnp.concatenate([lax.dynamic_slice_in_dim(value_rows, starts[level], caps[level], 0) for level in range(depth + 1)], 0)
        own_first = starts[-1]
        query_part = lax.dynamic_slice_in_dim(query_rows, own_first, own_cap, 0)
        grad_part = lax.dynamic_slice_in_dim(attn_grad, own_first, own_cap, 0)
        place = jnp.arange(own_cap, dtype=jnp.int32)
        live = place < seg_length[index]
        causal = place[None, :] <= place[:, None]
        allowed = jnp.concatenate([jnp.ones((own_cap, elder), dtype=bool), causal], 1) & live[:, None]
        attn, query_grad, key_grad, value_grad = segment_math(query_part, key_part, value_part, grad_part, allowed)
        attn_acc, query_acc, key_acc, value_acc = state
        attn_acc = add_rows(attn_acc, attn.astype(jnp.float32), own_first)
        query_acc = add_rows(query_acc, query_grad.astype(jnp.float32), own_first)
        begin = 0
        for level in range(depth + 1):
            key_acc = add_rows(key_acc, key_grad[begin:begin + caps[level]], starts[level])
            value_acc = add_rows(value_acc, value_grad[begin:begin + caps[level]], starts[level])
            begin = begin + caps[level]
        return (attn_acc, query_acc, key_acc, value_acc), None

    state, unused = lax.scan(one, state, indices)
    return state


def reference(query_rows, key_rows, value_rows, out_weight, out_grad, seg_owner, seg_parent, seg_offset, seg_length):
    attn_grad = jnp.dot(out_grad, out_weight.T, preferred_element_type=jnp.float32).astype(jnp.bfloat16)
    tree_base = jnp.arange(TREES, dtype=jnp.int32) * 21
    prompts = tree_base
    branches = (tree_base[:, None] + 1 + jnp.arange(4, dtype=jnp.int32)[None, :]).reshape(-1)
    leaves = (tree_base[:, None] + 5 + jnp.arange(16, dtype=jnp.int32)[None, :]).reshape(-1)
    state = (jnp.zeros((SLOTS, HEADS * HD), jnp.float32), jnp.zeros((SLOTS, HEADS * HD), jnp.float32),
             jnp.zeros((SLOTS, KV_HEADS * HD), jnp.float32), jnp.zeros((SLOTS, KV_HEADS * HD), jnp.float32))
    arrays = (query_rows, key_rows, value_rows, attn_grad, seg_owner, seg_parent, seg_offset, seg_length)
    for depth, indices in ((0, prompts), (1, branches), (2, leaves)):
        state = level_pass(state, indices, depth, arrays)
    attn_acc, query_acc, key_acc, value_acc = state
    attn = attn_acc.astype(jnp.bfloat16)
    layer_out = jnp.dot(attn, out_weight, preferred_element_type=jnp.float32).astype(jnp.bfloat16)
    attn_blocks = attn.reshape(N_LEAF, ROWS_DEV, HEADS * HD)
    grad_blocks = out_grad.reshape(N_LEAF, ROWS_DEV, D)

    def add_part(running, pair):
        part = lax.dot_general(pair[0], pair[1], (((0,), (0,)), ((), ())), preferred_element_type=jnp.float32).astype(jnp.bfloat16)
        return running + lax.optimization_barrier(part).astype(jnp.float32), None

    weight_sum, unused = lax.scan(add_part, jnp.zeros((HEADS * HD, D), jnp.float32), (attn_blocks, grad_blocks))
    return (layer_out, query_acc.astype(jnp.bfloat16), key_acc.astype(jnp.bfloat16),
            value_acc.astype(jnp.bfloat16), weight_sum.astype(jnp.bfloat16))
```

```python
import functools

import jax
import jax.numpy as jnp
from jax import lax
from jax.experimental import pallas as pl
from jax.experimental.pallas import tpu as pltpu
from jax.sharding import PartitionSpec as P

HD = 128
GROUP = 16
HEADS_DEV = 4
ROWS = 768
WIN = 128
ELDER = 512
TREE = 21
NEG = -1e30
SCALE = HD ** (-0.5)
VMEM = 60 * 1024 * 1024
F32 = jnp.float32
BF16 = jnp.bfloat16

SMEM_SPEC = pl.BlockSpec(memory_space=pltpu.SMEM)
VMEM_SPEC = pl.BlockSpec(memory_space=pltpu.VMEM)


def head_perm(array, dx, dy):
    pairs = [(h, ((h // 4 + dx) % 2) * 4 + (h + dy) % 4) for h in range(8)]
    return lax.ppermute(array, "head", pairs)


def leaf_perm(array, dz, dx, dc):
    pairs = [
        (l, ((l // 4 + dz) % 4) * 4 + ((l // 2 + dx) % 2) * 2 + (l + dc) % 2) for l in range(16)
    ]
    return lax.ppermute(array, "leaf", pairs)


def add(*parts):
    total = parts[0].astype(F32)
    for part in parts[1:]:
        total = total + part.astype(F32)
    return total.astype(BF16)


def pick(rows, side):
    return jnp.where(side == 0, rows[:, :HD], rows[:, HD:])


def elder_start(offset):
    return jnp.minimum(offset, ROWS - ELDER)


def pack_kernel(place, owner, offset, key_ref, value_ref, own_ref, elder_ref):
    leaf, side = place[0], place[1] // 4
    own_ref[:, :HD] = pick(key_ref[...], side)
    own_ref[:, HD:] = pick(value_ref[...], side)

    def find(i, start):
        mine = (owner[i] == leaf) & (i % TREE < 5)
        return jnp.where(mine, elder_start(offset[i]), start)

    start = lax.fori_loop(0, owner.shape[0], find, jnp.int32(0))
    elder_ref[...] = own_ref[pl.ds(pl.multiple_of(start, WIN), ELDER), :]


def pack(place, owner, offset, key_rows, value_rows):
    return pl.pallas_call(
        pack_kernel,
        out_shape=(
            jax.ShapeDtypeStruct((ROWS, 2 * HD), BF16),
            jax.ShapeDtypeStruct((ELDER, 2 * HD), BF16),
        ),
        in_specs=[SMEM_SPEC] * 3 + [VMEM_SPEC] * 2,
        out_specs=(VMEM_SPEC, VMEM_SPEC),
        compiler_params=pltpu.CompilerParams(vmem_limit_bytes=VMEM),
        cost_estimate=pl.CostEstimate(flops=0, bytes_accessed=2_000_000, transcendentals=0),
        name="pack_keys",
    )(place, owner, offset, key_rows, value_rows)


def relative_leaf(leaf, other):
    core = (leaf + other) % 2
    cross = (leaf // 2 + other // 2) % 2
    depth = (other // 4 - leaf // 4 + 4) % 4
    return core * 8 + depth * 2 + cross


def fill_table(table, place, owner, parent, offset, length):
    leaf = place[0]
    for w in range(ROWS // WIN):
        table[w, 0] = -1

    def first_rows(segment):
        shift = offset[segment] - elder_start(offset[segment])
        base = owner[segment] * ELDER + shift
        target = relative_leaf(leaf, owner[segment]) * ELDER + shift
        return base, target

    def visit(i, unused):
        @pl.when(owner[i] == leaf)
        def _():
            level = i % TREE
            prompt = i - level
            branch = jnp.where(level >= 5, parent[i], i)
            prompt_base, prompt_target = first_rows(prompt)
            branch_base, branch_target = first_rows(branch)
            tiles = jnp.where(level == 0, 4, jnp.where(level < 5, 2, 1))
            first = jnp.where(level == 0, 0, jnp.where(level < 5, 4, 6))
            window = offset[i] // WIN
            for j in range(4):

                @pl.when(j < tiles)
                def _():
                    table[window + j, 0] = first + j
                    table[window + j, 1] = length[i] - j * WIN
                    table[window + j, 2] = prompt_base
                    table[window + j, 3] = branch_base
                    table[window + j, 4] = prompt_target
                    table[window + j, 5] = branch_target

        return unused

    lax.fori_loop(0, owner.shape[0], visit, 0)


def heads_down(block):
    return jnp.concatenate([block[:, h * HD : (h + 1) * HD] for h in range(HEADS_DEV)], axis=0)


def tile_base(table, w, column, t):
    base = table[w, column] + t * WIN if t < 4 else table[w, column + 1] + (t - 4) * WIN
    return pl.multiple_of(base, WIN)


def for_windows(table, empty, full):
    def window(w, unused):
        count = table[w, 0]
        rows = pl.ds(pl.multiple_of(w * WIN, WIN), WIN)
        for low, high in ((-1, -1), (0, 3), (4, 5), (6, 6)):

            @pl.when((count >= low) & (count <= high))
            def _(high=high):
                if high < 0:
                    empty(w, rows)
                else:
                    full(w, rows, high, count)

        return unused

    lax.fori_loop(0, ROWS // WIN, window, 0)


def load_tiles(table, w, rows, tiles, gathered_ref, own_ref, pair_buf):
    for t in range(tiles):
        pair_buf[t * WIN : (t + 1) * WIN, :] = gathered_ref[
            pl.ds(tile_base(table, w, 2, t), WIN), :
        ]
    pair_buf[tiles * WIN : (tiles + 1) * WIN, :] = own_ref[rows, :]


def masked(scores, tiles, count):
    shape = scores.shape
    col = lax.broadcasted_iota(jnp.int32, shape, 1)
    row = lax.broadcasted_iota(jnp.int32, shape, 0) % WIN
    seen = (col < count * WIN) | ((col >= tiles * WIN) & (col - tiles * WIN <= row))
    return jnp.where(seen, scores, NEG)


def live_rows(table, w):
    row = lax.broadcasted_iota(jnp.int32, (HEADS_DEV * WIN, 1), 0) % WIN
    return (row < table[w, 1]).astype(F32)


def scores_of(query, keys):
    return lax.dot_general(query, keys, (((1,), (1,)), ((), ())), preferred_element_type=F32)


def forward_kernel(
    place, owner, parent, offset, length, query_ref, own_ref, gathered_ref, attn_ref, stat_ref,
    table, pair_buf,
):
    fill_table(table, place, owner, parent, offset, length)

    def empty(w, rows):
        attn_ref[rows, :] = jnp.zeros((WIN, HEADS_DEV * HD), BF16)
        stat_ref[rows, :] = jnp.zeros((WIN, HD), F32)

    def full(w, rows, tiles, count):
        load_tiles(table, w, rows, tiles, gathered_ref, own_ref, pair_buf)
        span = (tiles + 1) * WIN
        query = heads_down(query_ref[rows, :])
        scores = masked(scores_of(query, pair_buf[:span, :HD]) * SCALE, tiles, count)
        top = jnp.max(scores, axis=1, keepdims=True)
        weights = jnp.exp(scores - top)
        total = jnp.sum(weights, axis=1, keepdims=True)
        probs = (weights * (live_rows(table, w) / total)).astype(BF16)
        attn = jnp.dot(probs, pair_buf[:span, HD:], preferred_element_type=F32).astype(BF16)
        stat = top + jnp.log(total)
        lane = lax.broadcasted_iota(jnp.int32, (WIN, HD), 1)
        packed = jnp.zeros((WIN, HD), F32)
        for h in range(HEADS_DEV):
            part = slice(h * WIN, (h + 1) * WIN)
            attn_ref[rows, h * HD : (h + 1) * HD] = attn[part]
            packed = jnp.where(lane == h, stat[part], packed)
        stat_ref[rows, :] = packed

    for_windows(table, empty, full)


def forward(place, segs, query_rows, own, gathered):
    return pl.pallas_call(
        forward_kernel,
        out_shape=(
            jax.ShapeDtypeStruct((ROWS, HEADS_DEV * HD), BF16),
            jax.ShapeDtypeStruct((ROWS, HD), F32),
        ),
        in_specs=[SMEM_SPEC] * 5 + [VMEM_SPEC] * 3,
        out_specs=(VMEM_SPEC, VMEM_SPEC),
        scratch_shapes=[pltpu.SMEM((6, 8), jnp.int32), pltpu.VMEM((7 * WIN, 2 * HD), BF16)],
        compiler_params=pltpu.CompilerParams(vmem_limit_bytes=VMEM),
        cost_estimate=pl.CostEstimate(
            flops=2_000_000_000, bytes_accessed=8_000_000, transcendentals=2_000_000
        ),
        name="attention",
    )(place, *segs, query_rows, own, gathered)


def relative_head(head, k):
    return ((head // 4 + k // 4) % 2) * 4 + (head + k) % 4


def project_kernel(place, attn_ref, weight_ref, *rest):
    outs, ordered = rest[:8], rest[8]

    @pl.when(pl.program_id(0) == 0)
    def _():
        for k in range(8):
            first = pl.multiple_of(relative_head(place[1], k) * 96, 32)
            ordered[k * 96 : (k + 1) * 96, :] = attn_ref[pl.ds(first, 96), :]

    product = jnp.dot(ordered[...], weight_ref[...], preferred_element_type=F32).astype(BF16)
    for k in range(8):
        outs[k][...] = product[k * 96 : (k + 1) * 96, :]


def project(place, attn, out_weight):
    width = out_weight.shape[1]
    step = 512
    return pl.pallas_call(
        project_kernel,
        grid=(width // step,),
        out_shape=[jax.ShapeDtypeStruct((96, width), BF16)] * 8,
        in_specs=[
            SMEM_SPEC,
            pl.BlockSpec((ROWS, HEADS_DEV * HD), lambda n: (0, 0)),
            pl.BlockSpec((HEADS_DEV * HD, step), lambda n: (0, n)),
        ],
        out_specs=[pl.BlockSpec((96, step), lambda n: (0, n))] * 8,
        scratch_shapes=[pltpu.VMEM((ROWS, HEADS_DEV * HD), BF16)],
        compiler_params=pltpu.CompilerParams(vmem_limit_bytes=VMEM),
        cost_estimate=pl.CostEstimate(
            flops=3_200_000_000, bytes_accessed=11_000_000, transcendentals=0
        ),
        name="project",
    )(place, attn, out_weight)


def absolute_leaf(leaf, n):
    core = (leaf + 1 - n // 8) % 2
    depth = (leaf // 4 + (n % 8) // 2) % 4
    cross = (leaf // 2 + n % 2) % 2
    return depth * 4 + cross * 2 + core


def dense_back_kernel(place, attn_ref, weight_ref, *rest):
    pieces, outs, scratch = rest[:8], rest[8:11], rest[11:]
    grad_ref, other_ref, mine_ref = outs
    turned, rows, total = scratch
    n = pl.program_id(0)

    @pl.when(n == 0)
    def _():
        turned[...] = attn_ref[...].T
        total[...] = jnp.zeros_like(total)

    for k in range(8):
        first = pl.multiple_of(relative_head(place[1], k) * 96, 32)
        rows[pl.ds(first, 96), :] = pieces[k][...]
    block = rows[...]
    part = jnp.dot(turned[...], block, preferred_element_type=F32).astype(BF16)

    @pl.when(n < 8)
    def _():
        other_ref[0] = part

    @pl.when(n >= 8)
    def _():
        mine_ref[0] = part

    total[...] += scores_of(block, weight_ref[...])

    @pl.when(n == 15)
    def _():
        grad_ref[...] = total[...].astype(BF16)


def dense_back(place, attn, out_weight, pieces):
    feats = HEADS_DEV * HD
    step = 256
    column = lambda n, place: (0, absolute_leaf(place[0], n))
    return pl.pallas_call(
        dense_back_kernel,
        grid_spec=pltpu.PrefetchScalarGridSpec(
            num_scalar_prefetch=1,
            grid=(16,),
            in_specs=[
                pl.BlockSpec((ROWS, feats), lambda n, place: (0, 0)),
                pl.BlockSpec((feats, step), column),
            ]
            + [pl.BlockSpec((96, step), column)] * 8,
            out_specs=[
                pl.BlockSpec((ROWS, feats), lambda n, place: (0, 0)),
                pl.BlockSpec((1, feats, step), lambda n, place: (jnp.minimum(n, 7), 0, 0)),
                pl.BlockSpec((1, feats, step), lambda n, place: (jnp.maximum(n - 8, 0), 0, 0)),
            ],
            scratch_shapes=[
                pltpu.VMEM((feats, ROWS), BF16),
                pltpu.VMEM((ROWS, step), BF16),
                pltpu.VMEM((ROWS, feats), F32),
            ],
        ),
        out_shape=[
            jax.ShapeDtypeStruct((ROWS, feats), BF16),
            jax.ShapeDtypeStruct((8, feats, step), BF16),
            jax.ShapeDtypeStruct((8, feats, step), BF16),
        ],
        compiler_params=pltpu.CompilerParams(vmem_limit_bytes=VMEM),
        cost_estimate=pl.CostEstimate(
            flops=6_400_000_000, bytes_accessed=16_000_000, transcendentals=0
        ),
        name="dense_back",
    )(place, attn, out_weight, *pieces)


def backward_kernel(
    place, owner, parent, offset, length, query_ref, grad_ref, attn_ref, stat_ref, own_ref,
    gathered_ref, query_grad_ref, own_grad_ref, mine_ref, other_ref, table, pair_buf, elder_sum,
):
    fill_table(table, place, owner, parent, offset, length)
    elder_sum[...] = jnp.zeros_like(elder_sum)

    def empty(w, rows):
        query_grad_ref[rows, :] = jnp.zeros((WIN, HEADS_DEV * HD), BF16)
        own_grad_ref[rows, :] = jnp.zeros((WIN, 2 * HD), F32)

    def full(w, rows, tiles, count):
        load_tiles(table, w, rows, tiles, gathered_ref, own_ref, pair_buf)
        span = (tiles + 1) * WIN
        query = heads_down(query_ref[rows, :])
        grad = heads_down(grad_ref[rows, :])
        attn = heads_down(attn_ref[rows, :])
        packed = stat_ref[rows, :]
        stat = jnp.concatenate([packed[:, h : h + 1] for h in range(HEADS_DEV)], axis=0)
        delta = jnp.sum(grad.astype(F32) * attn.astype(F32), axis=1, keepdims=True)
        keys, values = pair_buf[:span, :HD], pair_buf[:span, HD:]
        scores = masked(scores_of(query, keys) * SCALE, tiles, count)
        probs = jnp.exp(scores - stat) * live_rows(table, w)
        dprobs = scores_of(grad, values)
        dscores = (probs * ((dprobs - delta) * SCALE)).astype(BF16)
        probs = probs.astype(BF16)
        query_grad = jnp.dot(dscores, keys, preferred_element_type=F32).astype(BF16)
        for h in range(HEADS_DEV):
            query_grad_ref[rows, h * HD : (h + 1) * HD] = query_grad[h * WIN : (h + 1) * WIN]
        turn = (((0,), (0,)), ((), ()))
        key_grad = lax.dot_general(dscores, query, turn, preferred_element_type=F32)
        value_grad = lax.dot_general(probs, grad, turn, preferred_element_type=F32)
        for t in range(tiles):
            spot = pl.ds(tile_base(table, w, 4, t), WIN)
            part = slice(t * WIN, (t + 1) * WIN)
            elder_sum[spot, :HD] += key_grad[part]
            elder_sum[spot, HD:] += value_grad[part]
        own_grad_ref[rows, :HD] = key_grad[tiles * WIN :]
        own_grad_ref[rows, HD:] = value_grad[tiles * WIN :]

    for_windows(table, empty, full)
    mine_ref[...] = elder_sum[: 8 * ELDER, :].astype(BF16)
    other_ref[...] = elder_sum[8 * ELDER :, :].astype(BF16)


def backward(place, segs, query_rows, grad, attn, stat, own, gathered):
    return pl.pallas_call(
        backward_kernel,
        out_shape=(
            jax.ShapeDtypeStruct((ROWS, HEADS_DEV * HD), BF16),
            jax.ShapeDtypeStruct((ROWS, 2 * HD), F32),
            jax.ShapeDtypeStruct((8 * ELDER, 2 * HD), BF16),
            jax.ShapeDtypeStruct((8 * ELDER, 2 * HD), BF16),
        ),
        in_specs=[SMEM_SPEC] * 5 + [VMEM_SPEC] * 6,
        out_specs=(VMEM_SPEC,) * 4,
        scratch_shapes=[
            pltpu.SMEM((6, 8), jnp.int32),
            pltpu.VMEM((7 * WIN, 2 * HD), BF16),
            pltpu.VMEM((16 * ELDER, 2 * HD), F32),
        ],
        compiler_params=pltpu.CompilerParams(vmem_limit_bytes=VMEM),
        cost_estimate=pl.CostEstimate(
            flops=5_000_000_000, bytes_accessed=14_000_000, transcendentals=2_000_000
        ),
        name="attention_back",
    )(place, *segs, query_rows, grad, attn, stat, own, gathered)


def settle_kernel(place, owner, offset, own_ref, *rest):
    parts, outs, total = rest[:2], rest[2:6], rest[6]
    leaf, head = place[0], place[1]
    total[...] = own_ref[...]

    def find(i, start):
        mine = (owner[i] == leaf) & (i % TREE < 5)
        return jnp.where(mine, elder_start(offset[i]), start)

    start = lax.fori_loop(0, owner.shape[0], find, jnp.int32(0))
    spot = pl.ds(pl.multiple_of(start, WIN), ELDER)
    total[spot, :] += sum(part[...].astype(F32) for part in parts)
    for k in range(4):
        for side in range(2):
            first = pl.multiple_of(relative_head(head, side * 4 + k) * 96, 32)
            outs[k][side] = total[pl.ds(first, 96), :].astype(BF16)


def settle(place, owner, offset, own, parts):
    return pl.pallas_call(
        settle_kernel,
        out_shape=[jax.ShapeDtypeStruct((2, 96, 2 * HD), BF16)] * 4,
        in_specs=[SMEM_SPEC] * 3 + [VMEM_SPEC] * 3,
        out_specs=[VMEM_SPEC] * 4,
        scratch_shapes=[pltpu.VMEM((ROWS, 2 * HD), F32)],
        compiler_params=pltpu.CompilerParams(vmem_limit_bytes=VMEM),
        cost_estimate=pl.CostEstimate(flops=0, bytes_accessed=2_000_000, transcendentals=0),
        name="settle",
    )(place, owner, offset, own, *parts)


def gather_grad(rows):
    before = head_perm(rows, 0, 1)
    after = head_perm(rows, 0, -1)
    cross = head_perm(rows, 1, 0)
    half = rows.shape[0] // 2
    far = jnp.concatenate(
        [head_perm(before[:half], 0, 1), head_perm(after[half:], 0, -1)], axis=0
    )
    cross_before = head_perm(cross, 0, 1)
    cross_after = head_perm(cross, 0, -1)
    cross_far = head_perm(far, 1, 0)
    return [rows, after, far, before, cross, cross_after, cross_far, cross_before]


def scatter_rows(parts):
    near, up, far, down, cross, cross_up, cross_far, cross_down = parts
    half = near.shape[0] // 2
    from_down = head_perm(cross_up, 0, 1)
    from_up = head_perm(cross_down, 0, -1)
    from_cross = head_perm(cross_far, 1, 0)
    far = add(far, from_cross)
    cross = add(cross, from_down, from_up)
    first = head_perm(far[:half], 0, 1)
    second = head_perm(far[half:], 0, -1)
    last = head_perm(cross, 1, 0)
    up = jnp.concatenate([add(up[:half], first), up[half:]], axis=0)
    down = jnp.concatenate([down[:half], add(down[half:], second)], axis=0)
    return add(near, last, head_perm(up, 0, 1), head_perm(down, 0, -1))


def scatter_leaf(other, mine):
    rows = mine.shape[0] // 8
    joined = add(mine, leaf_perm(other, 0, 0, 1))
    received = [
        leaf_perm(joined[2 * rows * d : 2 * rows * (d + 1)], d, 0, 0) for d in range(1, 4)
    ]
    summed = add(joined[: 2 * rows], *received)
    return summed[:rows], leaf_perm(summed[rows:], 0, 1, 0)


def shards(
    query_rows, key_rows, value_rows, out_weight, out_grad, seg_owner, seg_parent, seg_offset,
    seg_length,
):
    place = jnp.stack([lax.axis_index("leaf"), lax.axis_index("head")]).astype(jnp.int32)
    side = lax.axis_index("head") // 4
    segs = (seg_owner, seg_parent, seg_offset, seg_length)
    own, elder = pack(place, seg_owner, seg_offset, key_rows, value_rows)
    gathered = lax.all_gather(elder, "leaf", axis=0, tiled=True)
    pieces = gather_grad(out_grad)
    attn, stat = forward(place, segs, query_rows, own, gathered)
    parts = project(place, attn, out_weight)
    layer_out = scatter_rows(parts)
    attn_grad, other_weight, mine_weight = dense_back(place, attn, out_weight, pieces)
    feats = attn.shape[1]
    weight_mine, weight_recv = scatter_leaf(
        other_weight.reshape(8 * feats, -1), mine_weight.reshape(8 * feats, -1)
    )
    weight_grad = add(weight_mine, weight_recv)
    query_grads, own_grad, mine_pair, other_pair = backward(
        place, segs, query_rows, attn_grad, attn, stat, own, gathered
    )
    pair_mine, pair_recv = scatter_leaf(other_pair, mine_pair)
    blocks = settle(
        place, seg_owner, seg_offset, own_grad, [pair_mine, pair_recv]
    )
    total = blocks[0].astype(F32)
    for k in range(1, 4):
        total = total + head_perm(blocks[k], 0, k).astype(F32)
    total = total.astype(BF16)
    near = total[0]
    far = head_perm(total[1], 1, 0)
    first = jnp.where(side == 0, near, far)
    second = jnp.where(side == 0, far, near)
    key_grads = jnp.concatenate([first[:, :HD], second[:, :HD]], axis=1)
    value_grads = jnp.concatenate([first[:, HD:], second[:, HD:]], axis=1)
    return layer_out, query_grads, key_grads, value_grads, weight_grad


def solution(mesh):
    return jax.shard_map(
        shards,
        mesh=mesh,
        in_specs=(
            P("leaf", "head"),
            P("leaf", None),
            P("leaf", None),
            P("head", None),
            P(("leaf", "head"), None),
            P(),
            P(),
            P(),
            P(),
        ),
        out_specs=(
            P(("leaf", "head"), None),
            P("leaf", "head"),
            P(("leaf", "head"), None),
            P(("leaf", "head"), None),
            P("head", "leaf"),
        ),
        check_vma=False,
    )
```

```python
import functools
import math

import jax
import jax.numpy as jnp
from jax import lax
from jax.experimental import pallas as pl
from jax.experimental.pallas import tpu as pltpu
from jax.sharding import PartitionSpec as P

HD = 128
GROUP = 16
HEADS_DEV = 4
ROWS = 768
WIN = 128
ELDER = 512
TREE = 21
NEG = -1e30
SCALE = HD ** (-0.5)
SCALE2 = SCALE * math.log2(math.e)
VMEM = 60 * 1024 * 1024
F32 = jnp.float32
BF16 = jnp.bfloat16

Y_GROUPS = [[0, 1, 2, 3], [4, 5, 6, 7]]
Z_GROUPS = [[0, 4, 8, 12], [1, 5, 9, 13], [2, 6, 10, 14], [3, 7, 11, 15]]
SMEM_SPEC = pl.BlockSpec(memory_space=pltpu.SMEM)
VMEM_SPEC = pl.BlockSpec(memory_space=pltpu.VMEM)


def head_perm(array, dx, dy):
    pairs = [(h, ((h // 4 + dx) % 2) * 4 + (h + dy) % 4) for h in range(8)]
    return lax.ppermute(array, "head", pairs)


def leaf_perm(array, dz, dx, dc):
    pairs = [
        (l, ((l // 4 + dz) % 4) * 4 + ((l // 2 + dx) % 2) * 2 + (l + dc) % 2) for l in range(16)
    ]
    return lax.ppermute(array, "leaf", pairs)


def after(array, *others):
    return lax.optimization_barrier((array, *others))[0]


def add(*parts):
    total = parts[0].astype(F32)
    for part in parts[1:]:
        total = total + part.astype(F32)
    return total.astype(BF16)


def pick(rows, side):
    return jnp.where(side == 0, rows[:, :HD], rows[:, HD:])


def elder_start(offset):
    return jnp.minimum(offset, ROWS - ELDER)


def pack_kernel(place, owner, offset, key_ref, value_ref, own_ref, elder_ref):
    leaf, side = place[0], place[1] // 4
    own_ref[:, :HD] = pick(key_ref[...], side)
    own_ref[:, HD:] = pick(value_ref[...], side)

    def find(i, start):
        mine = (owner[i] == leaf) & (i % TREE < 5)
        return jnp.where(mine, elder_start(offset[i]), start)

    start = lax.fori_loop(0, owner.shape[0], find, jnp.int32(0))
    elder_ref[...] = own_ref[pl.ds(pl.multiple_of(start, WIN), ELDER), :]


def pack(place, owner, offset, key_rows, value_rows):
    return pl.pallas_call(
        pack_kernel,
        out_shape=(
            jax.ShapeDtypeStruct((ROWS, 2 * HD), BF16),
            jax.ShapeDtypeStruct((ELDER, 2 * HD), BF16),
        ),
        in_specs=[SMEM_SPEC] * 3 + [VMEM_SPEC] * 2,
        out_specs=(VMEM_SPEC, VMEM_SPEC),
        compiler_params=pltpu.CompilerParams(vmem_limit_bytes=VMEM),
        cost_estimate=pl.CostEstimate(flops=0, bytes_accessed=100_000, transcendentals=0),
        name="pack_keys",
    )(place, owner, offset, key_rows, value_rows)


def relative_leaf(leaf, other):
    core = (leaf + other) % 2
    cross = (leaf // 2 + other // 2) % 2
    return core * 8 + other // 4 * 2 + cross


def fill_table(table, place, owner, parent, offset, length):
    leaf = place[0]
    for w in range(ROWS // WIN):
        table[w, 0] = -1

    def first_row(segment):
        shift = offset[segment] - elder_start(offset[segment])
        return relative_leaf(leaf, owner[segment]) * ELDER + shift

    def visit(i, unused):
        @pl.when(owner[i] == leaf)
        def _():
            level = i % TREE
            prompt = i - level
            branch = jnp.where(level >= 5, parent[i], i)
            prompt_base = first_row(prompt)
            branch_base = first_row(branch)
            tiles = jnp.where(level == 0, 4, jnp.where(level < 5, 2, 1))
            first = jnp.where(level == 0, 0, jnp.where(level < 5, 4, 6))
            window = offset[i] // WIN
            for j in range(4):

                @pl.when(j < tiles)
                def _():
                    table[window + j, 0] = first + j
                    table[window + j, 1] = length[i] - j * WIN
                    table[window + j, 2] = prompt_base
                    table[window + j, 3] = branch_base

        return unused

    lax.fori_loop(0, owner.shape[0], visit, 0)


def heads_down(block):
    return jnp.concatenate([block[:, h * HD : (h + 1) * HD] for h in range(HEADS_DEV)], axis=0)


def tile_base(table, w, t):
    base = table[w, 2] + t * WIN if t < 4 else table[w, 3] + (t - 4) * WIN
    return pl.multiple_of(base, WIN)


def for_windows(table, empty, full):
    def window(w, unused):
        count = table[w, 0]
        rows = pl.ds(pl.multiple_of(w * WIN, WIN), WIN)
        for tiles in range(-1, 7):

            @pl.when(count == tiles)
            def _(tiles=tiles):
                if tiles < 0:
                    empty(w, rows)
                else:
                    full(w, rows, tiles)

        return unused

    lax.fori_loop(0, ROWS // WIN, window, 0)


def load_tiles(table, w, rows, tiles, mine_ref, other_ref, own_ref, pair_buf):
    half = 8 * ELDER
    for t in range(tiles):
        base = tile_base(table, w, t)
        spot = pl.ds(pl.multiple_of(base % half, WIN), WIN)
        pair_buf[t * WIN : (t + 1) * WIN, :] = jnp.where(
            base < half, mine_ref[spot, :], other_ref[spot, :]
        )
    pair_buf[tiles * WIN : (tiles + 1) * WIN, :] = own_ref[rows, :]


def masked(scores, tiles, fill):
    own = scores[:, tiles * WIN :]
    col = lax.broadcasted_iota(jnp.int32, own.shape, 1)
    row = lax.broadcasted_iota(jnp.int32, own.shape, 0) % WIN
    own = jnp.where(col <= row, own, fill)
    return jnp.concatenate([scores[:, : tiles * WIN], own], axis=1) if tiles else own


def live_rows(table, w):
    row = lax.broadcasted_iota(jnp.int32, (HEADS_DEV * WIN, 1), 0) % WIN
    return row < table[w, 1]


def scores_of(query, keys):
    return lax.dot_general(query, keys, (((1,), (1,)), ((), ())), preferred_element_type=F32)


def forward_kernel(
    place, owner, parent, offset, length, query_ref, own_ref, elder_mine_ref,
    elder_other_ref, attn_ref, stat_ref, table, pair_buf,
):
    fill_table(table, place, owner, parent, offset, length)

    def empty(w, rows):
        attn_ref[rows, :] = jnp.zeros((WIN, HEADS_DEV * HD), BF16)
        stat_ref[rows, :] = jnp.zeros((WIN, HD), F32)

    def full(w, rows, tiles):
        load_tiles(table, w, rows, tiles, elder_mine_ref, elder_other_ref, own_ref, pair_buf)
        span = (tiles + 1) * WIN
        query = heads_down(query_ref[rows, :])
        scores = masked(scores_of(query, pair_buf[:span, :HD]), tiles, NEG)
        top = jnp.max(scores, axis=1, keepdims=True)
        weights = jnp.exp2((scores - top) * SCALE2)
        total = jnp.sum(weights, axis=1, keepdims=True)
        live = live_rows(table, w)
        attn = jnp.dot(weights.astype(BF16), pair_buf[:span, HD:], preferred_element_type=F32)
        attn = (attn * jnp.where(live, 1.0 / total, 0.0)).astype(BF16)
        stat = jnp.where(live, top * SCALE2 + jnp.log2(total), -NEG)
        lane = lax.broadcasted_iota(jnp.int32, (WIN, HD), 1)
        packed = jnp.zeros((WIN, HD), F32)
        for h in range(HEADS_DEV):
            part = slice(h * WIN, (h + 1) * WIN)
            attn_ref[rows, h * HD : (h + 1) * HD] = attn[part]
            packed = jnp.where(lane == h, stat[part], packed)
        stat_ref[rows, :] = packed

    for_windows(table, empty, full)


def forward(place, segs, query_rows, own, elders):
    return pl.pallas_call(
        forward_kernel,
        out_shape=(
            jax.ShapeDtypeStruct((ROWS, HEADS_DEV * HD), BF16),
            jax.ShapeDtypeStruct((ROWS, HD), F32),
        ),
        in_specs=[SMEM_SPEC] * 5 + [VMEM_SPEC] * 4,
        out_specs=(VMEM_SPEC, VMEM_SPEC),
        scratch_shapes=[pltpu.SMEM((6, 8), jnp.int32), pltpu.VMEM((7 * WIN, 2 * HD), BF16)],
        compiler_params=pltpu.CompilerParams(vmem_limit_bytes=VMEM),
        cost_estimate=pl.CostEstimate(flops=0, bytes_accessed=100_000, transcendentals=0),
        name="attention",
    )(place, *segs, query_rows, own, *elders)


def relative_head(head, k):
    return ((head // 4 + k // 4) % 2) * 4 + (head + k) % 4


def project_kernel(attn_ref, weight_ref, out_ref):
    out_ref[...] = jnp.dot(attn_ref[...], weight_ref[...], preferred_element_type=F32).astype(BF16)


def project(attn, out_weight):
    width = out_weight.shape[1]
    step = 1024
    return pl.pallas_call(
        project_kernel,
        grid=(width // step,),
        out_shape=jax.ShapeDtypeStruct((ROWS, width), BF16),
        in_specs=[
            pl.BlockSpec((ROWS, HEADS_DEV * HD), lambda n: (0, 0)),
            pl.BlockSpec((HEADS_DEV * HD, step), lambda n: (0, n)),
        ],
        out_specs=pl.BlockSpec((ROWS, step), lambda n: (0, n)),
        compiler_params=pltpu.CompilerParams(vmem_limit_bytes=VMEM),
        cost_estimate=pl.CostEstimate(flops=0, bytes_accessed=100_000, transcendentals=0),
        name="project",
    )(attn, out_weight)


def attn_grad_kernel(place, weight_ref, *refs):
    pieces, grad_ref, rows, total = refs[:8], *refs[8:]
    n = pl.program_id(0)
    for k in range(8):
        first = pl.multiple_of(relative_head(place[1], k) * 96, 32)
        rows[pl.ds(first, 96), :] = pieces[k][...]
    part = scores_of(rows[...], weight_ref[...])

    @pl.when(n == 0)
    def _():
        total[...] = part

    @pl.when(n > 0)
    def _():
        total[...] += part

    @pl.when(n == pl.num_programs(0) - 1)
    def _():
        grad_ref[...] = total[...].astype(BF16)


def attn_grad_of(place, out_weight, pieces):
    feats, width = out_weight.shape
    step = 1024
    return pl.pallas_call(
        attn_grad_kernel,
        grid=(width // step,),
        out_shape=jax.ShapeDtypeStruct((ROWS, feats), BF16),
        in_specs=[SMEM_SPEC, pl.BlockSpec((feats, step), lambda n: (0, n))]
        + [pl.BlockSpec((96, step), lambda n: (0, n))] * 8,
        out_specs=pl.BlockSpec((ROWS, feats), lambda n: (0, 0)),
        scratch_shapes=[pltpu.VMEM((ROWS, step), BF16), pltpu.VMEM((ROWS, feats), F32)],
        compiler_params=pltpu.CompilerParams(vmem_limit_bytes=VMEM),
        cost_estimate=pl.CostEstimate(flops=0, bytes_accessed=100_000, transcendentals=0),
        name="attn_grad",
    )(place, out_weight, *pieces)


def weight_grad_kernel(place, attn_ref, *rest):
    pieces, mine_ref, other_ref, turned, rows = rest[:8], *rest[8:]
    leaf = place[0]

    @pl.when(pl.program_id(0) == 0)
    def _():
        turned[...] = attn_ref[...].T

    for k in range(8):
        first = pl.multiple_of(relative_head(place[1], k) * 96, 32)
        rows[pl.ds(first, 96), :] = pieces[k][...]
    product = jnp.dot(turned[...], rows[...], preferred_element_type=F32).astype(BF16)
    for j in range(4):
        part = product[:, j * 256 : (j + 1) * 256]
        cross = (leaf // 2 + j // 2) % 2

        @pl.when(leaf % 2 == j % 2)
        def _():
            mine_ref[cross] = part

        @pl.when(leaf % 2 != j % 2)
        def _():
            other_ref[cross] = part


def weight_grad_of(place, attn, pieces):
    feats, width = HEADS_DEV * HD, pieces[0].shape[1]
    step = width // 4
    return pl.pallas_call(
        weight_grad_kernel,
        grid=(4,),
        in_specs=[SMEM_SPEC, pl.BlockSpec((ROWS, feats), lambda n: (0, 0))]
        + [pl.BlockSpec((96, step), lambda n: (0, n))] * 8,
        out_specs=[pl.BlockSpec((2, feats, step // 4), lambda n: (n, 0, 0))] * 2,
        scratch_shapes=[pltpu.VMEM((feats, ROWS), BF16), pltpu.VMEM((ROWS, step), BF16)],
        out_shape=[jax.ShapeDtypeStruct((8, feats, step // 4), BF16)] * 2,
        compiler_params=pltpu.CompilerParams(vmem_limit_bytes=VMEM),
        cost_estimate=pl.CostEstimate(flops=0, bytes_accessed=100_000, transcendentals=0),
        name="weight_grad",
    )(place, attn, *pieces)


def backward_kernel(
    place, owner, parent, offset, length, query_ref, grad_ref, attn_ref, stat_ref, own_ref,
    elder_mine_ref, elder_other_ref, query_grad_ref, own_grad_ref, mine_ref, other_ref, table,
    pair_buf, elder_sum,
):
    fill_table(table, place, owner, parent, offset, length)
    elder_sum[...] = jnp.zeros_like(elder_sum)

    def empty(w, rows):
        query_grad_ref[rows, :] = jnp.zeros((WIN, HEADS_DEV * HD), BF16)
        own_grad_ref[rows, :] = jnp.zeros((WIN, 2 * HD), F32)

    def full(w, rows, tiles):
        load_tiles(table, w, rows, tiles, elder_mine_ref, elder_other_ref, own_ref, pair_buf)
        span = (tiles + 1) * WIN
        query = heads_down(query_ref[rows, :])
        grad = heads_down(grad_ref[rows, :])
        attn = heads_down(attn_ref[rows, :])
        packed = stat_ref[rows, :]
        stat = jnp.concatenate([packed[:, h : h + 1] for h in range(HEADS_DEV)], axis=0)
        delta = jnp.sum(grad.astype(F32) * attn.astype(F32), axis=1, keepdims=True)
        keys, values = pair_buf[:span, :HD], pair_buf[:span, HD:]
        probs = jnp.exp2(masked(scores_of(query, keys) * SCALE2 - stat, tiles, NEG))
        dprobs = scores_of(grad, values)
        dscores = (probs * (dprobs - delta)).astype(BF16)
        probs = probs.astype(BF16)
        query_grad = jnp.dot(dscores, keys, preferred_element_type=F32)
        query_grad = (query_grad * SCALE).astype(BF16)
        for h in range(HEADS_DEV):
            query_grad_ref[rows, h * HD : (h + 1) * HD] = query_grad[h * WIN : (h + 1) * WIN]
        turn = (((0,), (0,)), ((), ()))
        key_grad = SCALE * lax.dot_general(dscores, query, turn, preferred_element_type=F32)
        value_grad = lax.dot_general(probs, grad, turn, preferred_element_type=F32)
        for t in range(tiles):
            spot = pl.ds(tile_base(table, w, t), WIN)
            part = slice(t * WIN, (t + 1) * WIN)
            elder_sum[spot, :HD] += key_grad[part]
            elder_sum[spot, HD:] += value_grad[part]
        own_grad_ref[rows, :HD] = key_grad[tiles * WIN :]
        own_grad_ref[rows, HD:] = value_grad[tiles * WIN :]

    for_windows(table, empty, full)
    mine_ref[...] = elder_sum[: 8 * ELDER, :].astype(BF16)
    other_ref[...] = elder_sum[8 * ELDER :, :].astype(BF16)


def backward(place, segs, query_rows, grad, attn, stat, own, elders):
    return pl.pallas_call(
        backward_kernel,
        out_shape=(
            jax.ShapeDtypeStruct((ROWS, HEADS_DEV * HD), BF16),
            jax.ShapeDtypeStruct((ROWS, 2 * HD), F32),
            jax.ShapeDtypeStruct((8 * ELDER, 2 * HD), BF16),
            jax.ShapeDtypeStruct((8 * ELDER, 2 * HD), BF16),
        ),
        in_specs=[SMEM_SPEC] * 5 + [VMEM_SPEC] * 7,
        out_specs=(VMEM_SPEC,) * 4,
        scratch_shapes=[
            pltpu.SMEM((6, 8), jnp.int32),
            pltpu.VMEM((7 * WIN, 2 * HD), BF16),
            pltpu.VMEM((16 * ELDER, 2 * HD), F32),
        ],
        compiler_params=pltpu.CompilerParams(vmem_limit_bytes=VMEM),
        cost_estimate=pl.CostEstimate(flops=0, bytes_accessed=100_000, transcendentals=0),
        name="attention_back",
    )(place, *segs, query_rows, grad, attn, stat, own, *elders)


def settle_kernel(place, owner, offset, own_ref, *rest):
    parts, out_ref, total = rest[:2], rest[2], rest[3]
    leaf, head = place[0], place[1]
    total[...] = own_ref[...]

    def find(i, start):
        mine = (owner[i] == leaf) & (i % TREE < 5)
        return jnp.where(mine, elder_start(offset[i]), start)

    start = lax.fori_loop(0, owner.shape[0], find, jnp.int32(0))
    spot = pl.ds(pl.multiple_of(start, WIN), ELDER)
    total[spot, :] += sum(part[...].astype(F32) for part in parts)
    for y in range(4):
        for side in range(2):
            first = pl.multiple_of(((head // 4 + side) % 2 * 4 + y) * 96, 32)
            out_ref[y, side] = total[pl.ds(first, 96), :].astype(BF16)


def settle(place, owner, offset, own, parts):
    return pl.pallas_call(
        settle_kernel,
        out_shape=jax.ShapeDtypeStruct((4, 2, 96, 2 * HD), BF16),
        in_specs=[SMEM_SPEC] * 3 + [VMEM_SPEC] * 3,
        out_specs=VMEM_SPEC,
        scratch_shapes=[pltpu.VMEM((ROWS, 2 * HD), F32)],
        compiler_params=pltpu.CompilerParams(vmem_limit_bytes=VMEM),
        cost_estimate=pl.CostEstimate(flops=0, bytes_accessed=100_000, transcendentals=0),
        name="settle",
    )(place, owner, offset, own, *parts)


def exchange(blocks, axis, groups=None):
    return lax.all_to_all(blocks, axis, 0, 0, axis_index_groups=groups)


def spread_depth(blocks):
    depth = lax.axis_index("leaf") // 4
    ahead = [
        lax.dynamic_index_in_dim(blocks, (depth + d) % 4, 0, keepdims=False) for d in range(4)
    ]
    return [ahead[0], *[leaf_perm(ahead[d], d, 0, 0) for d in range(1, 4)]]


def sum_blocks(blocks):
    return add(*[blocks[i] for i in range(blocks.shape[0])])


def shards(
    query_rows, key_rows, value_rows, out_weight, out_grad, seg_owner, seg_parent, seg_offset,
    seg_length,
):
    place = jnp.stack([lax.axis_index("leaf"), lax.axis_index("head")]).astype(jnp.int32)
    side = lax.axis_index("head") // 4
    segs = (seg_owner, seg_parent, seg_offset, seg_length)
    own, elder = pack(place, seg_owner, seg_offset, key_rows, value_rows)
    pair = jnp.concatenate([elder, leaf_perm(elder, 0, 1, 0)], axis=0)

    rows = after(out_grad, pair)
    elder_mine = exchange(jnp.broadcast_to(pair, (4, *pair.shape)), "leaf", Z_GROUPS)
    before = head_perm(rows, 0, 1)
    behind = head_perm(rows, 0, -1)
    cross = head_perm(rows, 1, 0)
    elder_mine, before, behind, cross = lax.optimization_barrier(
        (elder_mine, before, behind, cross)
    )

    half = rows.shape[0] // 2
    far = jnp.concatenate(
        [head_perm(before[:half], 0, 1), head_perm(behind[half:], 0, -1)], axis=0
    )
    elder_mine = elder_mine.reshape(8 * ELDER, 2 * HD)
    elder_other = leaf_perm(elder_mine, 0, 0, 1)
    far, elder_other, cross = lax.optimization_barrier((far, elder_other, cross))

    cross_before = head_perm(cross, 0, 1)
    cross_behind = head_perm(cross, 0, -1)
    cross_far = head_perm(far, 1, 0)
    elders = (elder_mine, elder_other)
    attn, stat = forward(place, segs, query_rows, own, elders)
    partial = project(attn, out_weight)
    partial, cross_before, cross_behind, cross_far = lax.optimization_barrier(
        (partial, cross_before, cross_behind, cross_far)
    )

    pieces = [rows, behind, far, before, cross, cross_behind, cross_far, cross_before]
    layer_parts = exchange(partial.reshape(8, 96, -1), "head")
    attn_grad = attn_grad_of(place, after(out_weight, partial), pieces)
    query_grads, own_grad, mine_pair, other_pair = backward(
        place, segs, query_rows, attn_grad, attn, stat, own, elders
    )
    pair_recv = leaf_perm(other_pair, 0, 0, 1)
    mine_weight, other_weight = weight_grad_of(place, after(attn, other_pair), pieces)
    weight_recv = leaf_perm(other_weight, 0, 0, 1)
    pair_joined = add(after(mine_pair, other_weight), pair_recv)
    pair_parts = spread_depth(pair_joined.reshape(4, 2 * ELDER, 2 * HD))
    weight_joined = add(mine_weight, weight_recv)
    weight_joined = after(weight_joined, *pair_parts)
    weight_parts = spread_depth(weight_joined.reshape(4, 2, *weight_joined.shape[1:]))
    pair_sum = add(*pair_parts)
    pair_sum, layer_parts = lax.optimization_barrier((pair_sum, layer_parts))
    pair_last = leaf_perm(pair_sum[ELDER:], 0, 1, 0)
    layer_out = sum_blocks(layer_parts)
    blocks = settle(place, seg_owner, seg_offset, own_grad, [pair_sum[:ELDER], pair_last])
    weight_parts = [after(part, blocks) for part in weight_parts]
    weight_sum = add(*weight_parts)
    weight_grad = add(weight_sum[0], leaf_perm(weight_sum[1], 0, 1, 0))
    total = sum_blocks(exchange(blocks, "head", Y_GROUPS))
    near = total[0]
    far = head_perm(total[1], 1, 0)
    first = jnp.where(side == 0, near, far)
    second = jnp.where(side == 0, far, near)
    key_grads = jnp.concatenate([first[:, :HD], second[:, :HD]], axis=1)
    value_grads = jnp.concatenate([first[:, HD:], second[:, HD:]], axis=1)
    return layer_out, query_grads, key_grads, value_grads, weight_grad


def solution(mesh):
    return jax.shard_map(
        shards,
        mesh=mesh,
        in_specs=(
            P("leaf", "head"),
            P("leaf", None),
            P("leaf", None),
            P("head", None),
            P(("leaf", "head"), None),
            P(),
            P(),
            P(),
            P(),
        ),
        out_specs=(
            P(("leaf", "head"), None),
            P("leaf", "head"),
            P(("leaf", "head"), None),
            P(("leaf", "head"), None),
            P("head", "leaf"),
        ),
        check_vma=False,
    )
```

```python
import functools
import math

import jax
import jax.numpy as jnp
from jax import lax
from jax.experimental import pallas as pl
from jax.experimental.pallas import tpu as pltpu
from jax.sharding import PartitionSpec as P

HD = 128
GROUP = 16
HEADS_DEV = 4
ROWS = 768
WIN = 128
ELDER = 512
TREE = 21
SEEN = 2 * ELDER + 8 * 2 * WIN
NEG = -1e30
SCALE = HD ** (-0.5)
SCALE2 = SCALE * math.log2(math.e)
VMEM = 60 * 1024 * 1024
F32 = jnp.float32
BF16 = jnp.bfloat16

Y_GROUPS = [[0, 1, 2, 3], [4, 5, 6, 7]]
Z_GROUPS = [[0, 4, 8, 12], [1, 5, 9, 13], [2, 6, 10, 14], [3, 7, 11, 15]]
DOWN = (((0,), (0,)), ((), ()))
ANY_SPEC = pl.BlockSpec(memory_space=pl.ANY)
SMEM_SPEC = pl.BlockSpec(memory_space=pltpu.SMEM)
VMEM_SPEC = pl.BlockSpec(memory_space=pltpu.VMEM)


def head_perm(array, dx, dy):
    pairs = [(h, ((h // 4 + dx) % 2) * 4 + (h + dy) % 4) for h in range(8)]
    return lax.ppermute(array, "head", pairs)


def leaf_perm(array, dz, dx, dc):
    pairs = [
        (l, ((l // 4 + dz) % 4) * 4 + ((l // 2 + dx) % 2) * 2 + (l + dc) % 2) for l in range(16)
    ]
    return lax.ppermute(array, "leaf", pairs)


def after(array, *others):
    return lax.optimization_barrier((array, *others))[0]


def add(*parts):
    total = parts[0].astype(F32)
    for part in parts[1:]:
        total = total + part.astype(F32)
    return total.astype(BF16)


def pick(rows, side):
    return jnp.where(side == 0, rows[:, :HD], rows[:, HD:])


def elder_start(offset):
    return jnp.minimum(offset, ROWS - ELDER)


def pack_kernel(place, owner, offset, key_ref, value_ref, own_ref, elder_ref):
    leaf, side = place[0], place[1] // 4
    own_ref[:, :HD] = pick(key_ref[...], side)
    own_ref[:, HD:] = pick(value_ref[...], side)

    def find(i, start):
        mine = (owner[i] == leaf) & (i % TREE < 5)
        return jnp.where(mine, elder_start(offset[i]), start)

    start = lax.fori_loop(0, owner.shape[0], find, jnp.int32(0))
    elder_ref[...] = own_ref[pl.ds(pl.multiple_of(start, WIN), ELDER), :]


def pack(place, owner, offset, key_rows, value_rows):
    return pl.pallas_call(
        pack_kernel,
        out_shape=(
            jax.ShapeDtypeStruct((ROWS, 2 * HD), BF16),
            jax.ShapeDtypeStruct((ELDER, 2 * HD), BF16),
        ),
        in_specs=[SMEM_SPEC] * 3 + [VMEM_SPEC] * 2,
        out_specs=(VMEM_SPEC, VMEM_SPEC),
        compiler_params=pltpu.CompilerParams(vmem_limit_bytes=VMEM),
        cost_estimate=pl.CostEstimate(flops=0, bytes_accessed=100_000, transcendentals=0),
        name="pack_keys",
    )(place, owner, offset, key_rows, value_rows)


def empty_kernel(place, mine_ref, other_ref):
    del place
    mine_ref[...] = jnp.zeros_like(mine_ref)
    other_ref[...] = jnp.zeros_like(other_ref)


def empty_elders(place):
    return pl.pallas_call(
        empty_kernel,
        out_shape=[jax.ShapeDtypeStruct((8 * ELDER, 2 * HD), BF16)] * 2,
        in_specs=[SMEM_SPEC],
        out_specs=[VMEM_SPEC] * 2,
        compiler_params=pltpu.CompilerParams(vmem_limit_bytes=VMEM),
        cost_estimate=pl.CostEstimate(flops=0, bytes_accessed=100_000, transcendentals=0),
        name="empty_elders",
    )(place)


def relative_leaf(leaf, other):
    core = (leaf + other) % 2
    cross = (leaf // 2 + other // 2) % 2
    depth = (other // 4 - leaf // 4 + 4) % 4
    return core * 8 + depth * 2 + cross


def fill_table(table, place, owner, parent, offset, length):
    leaf = place[0]
    for w in range(ROWS // WIN):
        table[w, 0] = -1

    def first_row(segment):
        shift = offset[segment] - elder_start(offset[segment])
        return relative_leaf(leaf, owner[segment]) * ELDER + shift

    def visit(i, unused):
        @pl.when(owner[i] == leaf)
        def _():
            level = i % TREE
            prompt = i - level
            branch = jnp.where(level >= 5, parent[i], i)
            prompt_base = first_row(prompt)
            branch_base = first_row(branch)
            number = branch // TREE * 4 + branch % TREE - 1
            tiles = jnp.where(level == 0, 4, jnp.where(level < 5, 2, 1))
            first = jnp.where(level == 0, 0, jnp.where(level < 5, 4, 6))
            window = offset[i] // WIN
            for j in range(4):

                @pl.when(j < tiles)
                def _():
                    table[window + j, 0] = first + j
                    table[window + j, 1] = length[i] - j * WIN
                    table[window + j, 2] = prompt_base
                    table[window + j, 3] = branch_base
                    table[window + j, 4] = prompt // TREE * ELDER
                    table[window + j, 5] = 2 * ELDER + number * 2 * WIN

        return unused

    lax.fori_loop(0, owner.shape[0], visit, 0)


def heads_down(block):
    return jnp.concatenate([block[:, h * HD : (h + 1) * HD] for h in range(HEADS_DEV)], axis=0)


def tile_base(table, w, column, t):
    base = table[w, column] + t * WIN if t < 4 else table[w, column + 1] + (t - 4) * WIN
    return pl.multiple_of(base, WIN)


def for_windows(table, empty, full):
    def window(w, unused):
        count = table[w, 0]
        rows = pl.ds(pl.multiple_of(w * WIN, WIN), WIN)
        for tiles in range(-1, 7):

            @pl.when(count == tiles)
            def _(tiles=tiles):
                if tiles < 0:
                    empty(w, rows)
                else:
                    full(w, rows, tiles)

        return unused

    lax.fori_loop(0, ROWS // WIN, window, 0)


def start_tiles(table, mine_ref, other_ref, pair_buf, sems):
    half = 8 * ELDER

    def window(w, unused):
        for t in range(6):
            base = tile_base(table, w, 2, t)
            there = pair_buf.at[w, pl.ds(t * WIN, WIN), :]

            @pl.when((t < table[w, 0]) & (base < half))
            def _():
                source = mine_ref.at[pl.ds(base, WIN), :]
                pltpu.make_async_copy(source, there, sems.at[w]).start()

            @pl.when((t < table[w, 0]) & (base >= half))
            def _():
                source = other_ref.at[pl.ds(pl.multiple_of(base - half, WIN), WIN), :]
                pltpu.make_async_copy(source, there, sems.at[w]).start()

        return unused

    lax.fori_loop(0, ROWS // WIN, window, 0)


def wait_tiles(w, rows, tiles, mine_ref, own_ref, pair_buf, sems):
    span = tiles * WIN
    if tiles:
        spot = pair_buf.at[w, pl.ds(0, span), :]
        pltpu.make_async_copy(mine_ref.at[pl.ds(0, span), :], spot, sems.at[w]).wait()
    pair_buf[w, span : span + WIN, :] = own_ref[rows, :]
    return pair_buf[w, : span + WIN, :HD], pair_buf[w, : span + WIN, HD:]


def masked(scores, tiles):
    own = scores[tiles * WIN :, :]
    key = lax.broadcasted_iota(jnp.int32, own.shape, 0)
    query = lax.broadcasted_iota(jnp.int32, own.shape, 1) % WIN
    own = jnp.where(key <= query, own, NEG)
    return jnp.concatenate([scores[: tiles * WIN, :], own], axis=0) if tiles else own


def live_columns(table, w):
    place = lax.broadcasted_iota(jnp.int32, (1, HEADS_DEV * WIN), 1) % WIN
    return place < table[w, 1]


def scores_of(query, keys):
    return lax.dot_general(query, keys, (((1,), (1,)), ((), ())), preferred_element_type=F32)


def forward_kernel(
    place, owner, parent, offset, length, query_ref, own_ref, elder_mine_ref,
    elder_other_ref, attn_ref, stat_ref, table, pair_buf, sems,
):
    fill_table(table, place, owner, parent, offset, length)
    start_tiles(table, elder_mine_ref, elder_other_ref, pair_buf, sems)

    def empty(w, rows):
        attn_ref[rows, :] = jnp.zeros((WIN, HEADS_DEV * HD), BF16)

    def full(w, rows, tiles):
        keys, values = wait_tiles(w, rows, tiles, elder_mine_ref, own_ref, pair_buf, sems)
        query = heads_down(query_ref[rows, :])
        scores = masked(scores_of(keys, query), tiles)
        top = jnp.max(scores, axis=0, keepdims=True)
        weights = jnp.exp2((scores - top) * SCALE2)
        total = jnp.sum(weights, axis=0, keepdims=True)
        live = live_columns(table, w)
        attn = lax.dot_general(values, weights.astype(BF16), DOWN, preferred_element_type=F32)
        attn = (attn * jnp.where(live, 1.0 / total, 0.0)).astype(BF16).T
        stat_ref[w, 0:1, :] = jnp.where(live, top * SCALE2 + jnp.log2(total), -NEG)
        for h in range(HEADS_DEV):
            attn_ref[rows, h * HD : (h + 1) * HD] = attn[h * WIN : (h + 1) * WIN]

    for_windows(table, empty, full)


def forward(place, segs, query_rows, own, elders):
    return pl.pallas_call(
        forward_kernel,
        out_shape=(
            jax.ShapeDtypeStruct((ROWS, HEADS_DEV * HD), BF16),
            jax.ShapeDtypeStruct((ROWS // WIN, 8, HEADS_DEV * WIN), F32),
        ),
        in_specs=[SMEM_SPEC] * 5 + [VMEM_SPEC] * 2 + [ANY_SPEC] * 2,
        out_specs=(VMEM_SPEC, VMEM_SPEC),
        scratch_shapes=[
            pltpu.SMEM((6, 8), jnp.int32),
            pltpu.VMEM((6, 7 * WIN, 2 * HD), BF16),
            pltpu.SemaphoreType.DMA((6,)),
        ],
        compiler_params=pltpu.CompilerParams(vmem_limit_bytes=VMEM),
        cost_estimate=pl.CostEstimate(flops=0, bytes_accessed=100_000, transcendentals=0),
        name="attention",
    )(place, *segs, query_rows, own, *elders)


def relative_head(head, k):
    return ((head // 4 + k // 4) % 2) * 4 + (head + k) % 4


def project_kernel(attn_ref, weight_ref, out_ref):
    out_ref[...] = jnp.dot(attn_ref[...], weight_ref[...], preferred_element_type=F32).astype(BF16)


def project(attn, out_weight):
    width = out_weight.shape[1]
    step = 1024
    return pl.pallas_call(
        project_kernel,
        grid=(width // step,),
        out_shape=jax.ShapeDtypeStruct((ROWS, width), BF16),
        in_specs=[
            pl.BlockSpec((ROWS, HEADS_DEV * HD), lambda n: (0, 0)),
            pl.BlockSpec((HEADS_DEV * HD, step), lambda n: (0, n)),
        ],
        out_specs=pl.BlockSpec((ROWS, step), lambda n: (0, n)),
        compiler_params=pltpu.CompilerParams(vmem_limit_bytes=VMEM),
        cost_estimate=pl.CostEstimate(flops=0, bytes_accessed=100_000, transcendentals=0),
        name="project",
    )(attn, out_weight)


def attn_grad_kernel(place, weight_ref, *refs):
    pieces, grad_ref, rows, total = refs[:8], *refs[8:]
    n = pl.program_id(0)
    for k in range(8):
        first = pl.multiple_of(relative_head(place[1], k) * 96, 32)
        rows[pl.ds(first, 96), :] = pieces[k][...]
    part = scores_of(rows[...], weight_ref[...])

    @pl.when(n == 0)
    def _():
        total[...] = part

    @pl.when(n > 0)
    def _():
        total[...] += part

    @pl.when(n == pl.num_programs(0) - 1)
    def _():
        grad_ref[...] = total[...].astype(BF16)


def attn_grad_of(place, out_weight, pieces):
    feats, width = out_weight.shape
    step = 1024
    return pl.pallas_call(
        attn_grad_kernel,
        grid=(width // step,),
        out_shape=jax.ShapeDtypeStruct((ROWS, feats), BF16),
        in_specs=[SMEM_SPEC, pl.BlockSpec((feats, step), lambda n: (0, n))]
        + [pl.BlockSpec((96, step), lambda n: (0, n))] * 8,
        out_specs=pl.BlockSpec((ROWS, feats), lambda n: (0, 0)),
        scratch_shapes=[pltpu.VMEM((ROWS, step), BF16), pltpu.VMEM((ROWS, feats), F32)],
        compiler_params=pltpu.CompilerParams(vmem_limit_bytes=VMEM),
        cost_estimate=pl.CostEstimate(flops=0, bytes_accessed=100_000, transcendentals=0),
        name="attn_grad",
    )(place, out_weight, *pieces)


def weight_grad_kernel(flip, place, attn_ref, *rest):
    pieces, out_ref, turned, rows = rest[:8], *rest[8:]
    leaf = place[0]

    @pl.when(pl.program_id(0) == 0)
    def _():
        turned[...] = attn_ref[...].T

    for core in range(2):

        @pl.when((leaf + flip) % 2 == core)
        def _():
            for k in range(8):
                first = pl.multiple_of(relative_head(place[1], k) * 96, 32)
                for j in range(4):
                    begin = (j * 2 + core) * 256
                    rows[pl.ds(first, 96), j * 256 : (j + 1) * 256] = pieces[k][
                        :, begin : begin + 256
                    ]

    product = jnp.dot(turned[...], rows[...], preferred_element_type=F32).astype(BF16)
    for j in range(4):
        out_ref[j // 2 * 2 + (leaf // 2 + j) % 2] = product[:, j * 256 : (j + 1) * 256]


def weight_grad_of(place, attn, pieces, flip):
    feats, width = HEADS_DEV * HD, pieces[0].shape[1]
    step = width // 2
    return pl.pallas_call(
        functools.partial(weight_grad_kernel, flip),
        grid=(2,),
        in_specs=[SMEM_SPEC, pl.BlockSpec((ROWS, feats), lambda n: (0, 0))]
        + [pl.BlockSpec((96, step), lambda n: (0, n))] * 8,
        out_specs=pl.BlockSpec((4, feats, 256), lambda n: (n, 0, 0)),
        scratch_shapes=[pltpu.VMEM((feats, ROWS), BF16), pltpu.VMEM((ROWS, step // 2), BF16)],
        out_shape=jax.ShapeDtypeStruct((8, feats, 256), BF16),
        compiler_params=pltpu.CompilerParams(vmem_limit_bytes=VMEM),
        cost_estimate=pl.CostEstimate(flops=0, bytes_accessed=100_000, transcendentals=0),
        name="weight_grad",
    )(place, attn, *pieces)


def backward_kernel(
    place, owner, parent, offset, length, query_ref, grad_ref, attn_ref, stat_ref, own_ref,
    elder_mine_ref, elder_other_ref, zero_mine_ref, zero_other_ref, query_grad_ref, own_grad_ref,
    mine_ref, other_ref, table, pair_buf, elder_sum, elder_out, sems, out_sem,
):
    del zero_mine_ref, zero_other_ref
    fill_table(table, place, owner, parent, offset, length)
    start_tiles(table, elder_mine_ref, elder_other_ref, pair_buf, sems)
    elder_sum[...] = jnp.zeros_like(elder_sum)

    def empty(w, rows):
        query_grad_ref[rows, :] = jnp.zeros((WIN, HEADS_DEV * HD), BF16)
        own_grad_ref[rows, :] = jnp.zeros((WIN, 2 * HD), F32)

    def full(w, rows, tiles):
        keys, values = wait_tiles(w, rows, tiles, elder_mine_ref, own_ref, pair_buf, sems)
        query = heads_down(query_ref[rows, :])
        grad = heads_down(grad_ref[rows, :])
        attn = heads_down(attn_ref[rows, :])
        delta = jnp.sum((grad.astype(F32) * attn.astype(F32)).T, axis=0, keepdims=True)
        probs = jnp.exp2(masked(scores_of(keys, query) * SCALE2 - stat_ref[w, 0:1, :], tiles))
        dprobs = scores_of(values, grad)
        dscores = (probs * (dprobs - delta)).astype(BF16)
        query_grad = lax.dot_general(keys, dscores, DOWN, preferred_element_type=F32)
        query_grad = (query_grad * SCALE).astype(BF16).T
        for h in range(HEADS_DEV):
            query_grad_ref[rows, h * HD : (h + 1) * HD] = query_grad[h * WIN : (h + 1) * WIN]
        key_grad = SCALE * jnp.dot(dscores, query, preferred_element_type=F32)
        value_grad = jnp.dot(probs.astype(BF16), grad, preferred_element_type=F32)
        for t in range(tiles):
            spot = pl.ds(tile_base(table, w, 4, t), WIN)
            part = slice(t * WIN, (t + 1) * WIN)
            elder_sum[spot, :HD] += key_grad[part]
            elder_sum[spot, HD:] += value_grad[part]
        own_grad_ref[rows, :HD] = key_grad[tiles * WIN :]
        own_grad_ref[rows, HD:] = value_grad[tiles * WIN :]

    for_windows(table, empty, full)
    elder_out[...] = elder_sum[...].astype(BF16)
    half = 8 * ELDER
    for tree in range(2):
        for level in range(5):
            segment = tree * TREE + level
            count = ELDER if level == 0 else 2 * WIN
            first = tree * ELDER if level == 0 else 2 * ELDER + (tree * 4 + level - 1) * 2 * WIN
            shift = offset[segment] - elder_start(offset[segment])
            base = relative_leaf(place[0], owner[segment]) * ELDER + shift
            source = elder_out.at[pl.ds(first, count), :]

            @pl.when(base < half)
            def _():
                target = mine_ref.at[pl.ds(pl.multiple_of(base, WIN), count), :]
                pltpu.make_async_copy(source, target, out_sem).start()

            @pl.when(base >= half)
            def _():
                target = other_ref.at[pl.ds(pl.multiple_of(base - half, WIN), count), :]
                pltpu.make_async_copy(source, target, out_sem).start()

    pltpu.make_async_copy(elder_out, mine_ref.at[pl.ds(0, SEEN), :], out_sem).wait()


def backward(place, segs, query_rows, grad, attn, stat, own, elders, zeros):
    return pl.pallas_call(
        backward_kernel,
        out_shape=(
            jax.ShapeDtypeStruct((ROWS, HEADS_DEV * HD), BF16),
            jax.ShapeDtypeStruct((ROWS, 2 * HD), F32),
            jax.ShapeDtypeStruct((8 * ELDER, 2 * HD), BF16),
            jax.ShapeDtypeStruct((8 * ELDER, 2 * HD), BF16),
        ),
        in_specs=[SMEM_SPEC] * 5 + [VMEM_SPEC] * 5 + [ANY_SPEC] * 4,
        out_specs=(VMEM_SPEC, VMEM_SPEC, ANY_SPEC, ANY_SPEC),
        input_output_aliases={12: 2, 13: 3},
        scratch_shapes=[
            pltpu.SMEM((6, 8), jnp.int32),
            pltpu.VMEM((6, 7 * WIN, 2 * HD), BF16),
            pltpu.VMEM((SEEN, 2 * HD), F32),
            pltpu.VMEM((SEEN, 2 * HD), BF16),
            pltpu.SemaphoreType.DMA((6,)),
            pltpu.SemaphoreType.DMA,
        ],
        compiler_params=pltpu.CompilerParams(vmem_limit_bytes=VMEM),
        cost_estimate=pl.CostEstimate(flops=0, bytes_accessed=100_000, transcendentals=0),
        name="attention_back",
    )(place, *segs, query_rows, grad, attn, stat, own, *elders, *zeros)


def settle_kernel(place, owner, offset, own_ref, *rest):
    parts, out_ref, total = rest[:2], rest[2], rest[3]
    leaf, head = place[0], place[1]
    total[...] = own_ref[...]

    def find(i, start):
        mine = (owner[i] == leaf) & (i % TREE < 5)
        return jnp.where(mine, elder_start(offset[i]), start)

    start = lax.fori_loop(0, owner.shape[0], find, jnp.int32(0))
    spot = pl.ds(pl.multiple_of(start, WIN), ELDER)
    total[spot, :] += sum(part[...].astype(F32) for part in parts)
    for y in range(4):
        for side in range(2):
            first = pl.multiple_of(((head // 4 + side) % 2 * 4 + y) * 96, 32)
            out_ref[y, side] = total[pl.ds(first, 96), :].astype(BF16)


def settle(place, owner, offset, own, parts):
    return pl.pallas_call(
        settle_kernel,
        out_shape=jax.ShapeDtypeStruct((4, 2, 96, 2 * HD), BF16),
        in_specs=[SMEM_SPEC] * 3 + [VMEM_SPEC] * 3,
        out_specs=VMEM_SPEC,
        scratch_shapes=[pltpu.VMEM((ROWS, 2 * HD), F32)],
        compiler_params=pltpu.CompilerParams(vmem_limit_bytes=VMEM),
        cost_estimate=pl.CostEstimate(flops=0, bytes_accessed=100_000, transcendentals=0),
        name="settle",
    )(place, owner, offset, own, *parts)


def exchange(blocks, axis, groups=None):
    return lax.all_to_all(blocks, axis, 0, 0, axis_index_groups=groups)


def spread_depth(blocks):
    depth = lax.axis_index("leaf") // 4
    ahead = [
        lax.dynamic_index_in_dim(blocks, (depth + d) % 4, 0, keepdims=False) for d in range(4)
    ]
    return [ahead[0], *[leaf_perm(ahead[d], d, 0, 0) for d in range(1, 4)]]


def sum_blocks(blocks):
    return add(*[blocks[i] for i in range(blocks.shape[0])])


def shards(
    query_rows, key_rows, value_rows, out_weight, out_grad, seg_owner, seg_parent, seg_offset,
    seg_length,
):
    place = jnp.stack([lax.axis_index("leaf"), lax.axis_index("head")]).astype(jnp.int32)
    side = lax.axis_index("head") // 4
    segs = (seg_owner, seg_parent, seg_offset, seg_length)
    own, elder = pack(place, seg_owner, seg_offset, key_rows, value_rows)
    pair = jnp.concatenate([elder, leaf_perm(elder, 0, 1, 0)], axis=0)

    before = head_perm(out_grad, 0, 1)
    behind = head_perm(out_grad, 0, -1)
    cross = head_perm(out_grad, 1, 0)
    half = out_grad.shape[0] // 2
    far = jnp.concatenate(
        [head_perm(before[:half], 0, 1), head_perm(behind[half:], 0, -1)], axis=0
    )
    cross_before = head_perm(cross, 0, 1)
    cross_behind = head_perm(cross, 0, -1)
    zeros = empty_elders(after(place, pair))
    elder_mine = jnp.concatenate(
        [pair, *[leaf_perm(pair, -d, 0, 0) for d in range(1, 4)]], axis=0
    )
    elder_mine, far, cross_before, cross_behind, *zeros = lax.optimization_barrier(
        (elder_mine, far, cross_before, cross_behind, *zeros)
    )
    elder_other = leaf_perm(elder_mine, 0, 0, 1)
    cross_far = head_perm(far, 1, 0)
    elders = (elder_mine, elder_other)
    attn, stat = forward(place, segs, query_rows, own, elders)
    partial = project(attn, out_weight)
    partial, cross_far = lax.optimization_barrier((partial, cross_far))

    pieces = [out_grad, behind, far, before, cross, cross_behind, cross_far, cross_before]
    layer_parts = exchange(partial.reshape(8, 96, -1), "head")
    attn_grad = attn_grad_of(place, after(out_weight, partial), pieces)
    query_grads, own_grad, mine_pair, other_pair = backward(
        place, segs, query_rows, attn_grad, attn, stat, own, elders, zeros
    )
    pair_recv = leaf_perm(other_pair, 0, 0, 1)
    other_weight = weight_grad_of(place, after(attn, other_pair), pieces, 1)
    weight_recv = leaf_perm(other_weight, 0, 0, 1)
    pair_joined = add(after(mine_pair, other_weight), pair_recv)
    pair_blocks = pair_joined.reshape(4, 2 * ELDER, 2 * HD)
    pair_parts = [pair_blocks[0], *[leaf_perm(pair_blocks[d], d, 0, 0) for d in range(1, 4)]]
    mine_weight = weight_grad_of(place, after(attn, pair_joined), pieces, 0)
    weight_joined = add(mine_weight, weight_recv)
    weight_joined = after(weight_joined, *pair_parts)
    weight_parts = spread_depth(weight_joined.reshape(4, 2, *weight_joined.shape[1:]))
    pair_sum = add(*pair_parts)
    pair_sum, layer_parts = lax.optimization_barrier((pair_sum, layer_parts))
    pair_last = leaf_perm(pair_sum[ELDER:], 0, 1, 0)
    layer_out = sum_blocks(layer_parts)
    blocks = settle(place, seg_owner, seg_offset, own_grad, [pair_sum[:ELDER], pair_last])
    weight_parts = [after(part, blocks) for part in weight_parts]
    weight_sum = add(*weight_parts)
    weight_grad = add(weight_sum[0], leaf_perm(weight_sum[1], 0, 1, 0))
    total = sum_blocks(exchange(blocks, "head", Y_GROUPS))
    near = total[0]
    far = head_perm(total[1], 1, 0)
    first = jnp.where(side == 0, near, far)
    second = jnp.where(side == 0, far, near)
    key_grads = jnp.concatenate([first[:, :HD], second[:, :HD]], axis=1)
    value_grads = jnp.concatenate([first[:, HD:], second[:, HD:]], axis=1)
    return layer_out, query_grads, key_grads, value_grads, weight_grad


def solution(mesh):
    return jax.shard_map(
        shards,
        mesh=mesh,
        in_specs=(
            P("leaf", "head"),
            P("leaf", None),
            P("leaf", None),
            P("head", None),
            P(("leaf", "head"), None),
            P(),
            P(),
            P(),
            P(),
        ),
        out_specs=(
            P(("leaf", "head"), None),
            P("leaf", "head"),
            P(("leaf", "head"), None),
            P(("leaf", "head"), None),
            P("head", "leaf"),
        ),
        check_vma=False,
    )
```

```python
import functools
import math

import jax
import jax.numpy as jnp
from jax import lax
from jax.experimental import pallas as pl
from jax.experimental.pallas import tpu as pltpu
from jax.sharding import PartitionSpec as P

HD = 128
GROUP = 16
HEADS_DEV = 4
ROWS = 768
WIN = 128
ELDER = 512
TREE = 21
SEEN = 2 * ELDER + 8 * 2 * WIN
NEG = -1e30
SCALE = HD ** (-0.5)
SCALE2 = SCALE * math.log2(math.e)
VMEM = 60 * 1024 * 1024
F32 = jnp.float32
BF16 = jnp.bfloat16

Z_GROUPS = [[0, 4, 8, 12], [1, 5, 9, 13], [2, 6, 10, 14], [3, 7, 11, 15]]
DOWN = (((0,), (0,)), ((), ()))
ANY_SPEC = pl.BlockSpec(memory_space=pl.ANY)
SMEM_SPEC = pl.BlockSpec(memory_space=pltpu.SMEM)
VMEM_SPEC = pl.BlockSpec(memory_space=pltpu.VMEM)


def head_perm(array, dx, dy):
    pairs = [(h, ((h // 4 + dx) % 2) * 4 + (h + dy) % 4) for h in range(8)]
    return lax.ppermute(array, "head", pairs)


def leaf_perm(array, dz, dx, dc):
    pairs = [
        (l, ((l // 4 + dz) % 4) * 4 + ((l // 2 + dx) % 2) * 2 + (l + dc) % 2) for l in range(16)
    ]
    return lax.ppermute(array, "leaf", pairs)


def after(array, *others):
    return lax.optimization_barrier((array, *others))[0]


def add(*parts):
    total = parts[0].astype(F32)
    for part in parts[1:]:
        total = total + part.astype(F32)
    return total.astype(BF16)


def pick(rows, side):
    return jnp.where(side == 0, rows[:, :HD], rows[:, HD:])


def elder_start(offset):
    return jnp.minimum(offset, ROWS - ELDER)


def pack_kernel(place, owner, offset, key_ref, value_ref, own_ref, elder_ref):
    leaf, side = place[0], place[1] // 4
    own_ref[:, :HD] = pick(key_ref[...], side)
    own_ref[:, HD:] = pick(value_ref[...], side)

    def find(i, start):
        mine = (owner[i] == leaf) & (i % TREE < 5)
        return jnp.where(mine, elder_start(offset[i]), start)

    start = lax.fori_loop(0, owner.shape[0], find, jnp.int32(0))
    elder_ref[...] = own_ref[pl.ds(pl.multiple_of(start, WIN), ELDER), :]


def pack(place, owner, offset, key_rows, value_rows):
    return pl.pallas_call(
        pack_kernel,
        out_shape=(
            jax.ShapeDtypeStruct((ROWS, 2 * HD), BF16),
            jax.ShapeDtypeStruct((ELDER, 2 * HD), BF16),
        ),
        in_specs=[SMEM_SPEC] * 3 + [VMEM_SPEC] * 2,
        out_specs=(VMEM_SPEC, VMEM_SPEC),
        compiler_params=pltpu.CompilerParams(vmem_limit_bytes=VMEM),
        cost_estimate=pl.CostEstimate(flops=0, bytes_accessed=100_000, transcendentals=0),
        name="pack_keys",
    )(place, owner, offset, key_rows, value_rows)


def empty_kernel(place, mine_ref, other_ref):
    del place
    mine_ref[...] = jnp.zeros_like(mine_ref)
    other_ref[...] = jnp.zeros_like(other_ref)


def empty_elders(place):
    return pl.pallas_call(
        empty_kernel,
        out_shape=[jax.ShapeDtypeStruct((8 * ELDER, 2 * HD), BF16)] * 2,
        in_specs=[SMEM_SPEC],
        out_specs=[VMEM_SPEC] * 2,
        compiler_params=pltpu.CompilerParams(vmem_limit_bytes=VMEM),
        cost_estimate=pl.CostEstimate(flops=0, bytes_accessed=100_000, transcendentals=0),
        name="empty_elders",
    )(place)


def relative_leaf(leaf, other):
    core = (leaf + other) % 2
    cross = (leaf // 2 + other // 2) % 2
    depth = (other // 4 - leaf // 4 + 4) % 4
    return core * 8 + depth * 2 + cross


def fill_table(table, place, owner, parent, offset, length):
    leaf = place[0]
    for w in range(ROWS // WIN):
        table[w, 0] = -1

    def first_row(segment):
        shift = offset[segment] - elder_start(offset[segment])
        return relative_leaf(leaf, owner[segment]) * ELDER + shift

    def visit(i, unused):
        @pl.when(owner[i] == leaf)
        def _():
            level = i % TREE
            prompt = i - level
            branch = jnp.where(level >= 5, parent[i], i)
            prompt_base = first_row(prompt)
            branch_base = first_row(branch)
            number = branch // TREE * 4 + branch % TREE - 1
            tiles = jnp.where(level == 0, 4, jnp.where(level < 5, 2, 1))
            first = jnp.where(level == 0, 0, jnp.where(level < 5, 4, 6))
            window = offset[i] // WIN
            for j in range(4):

                @pl.when(j < tiles)
                def _():
                    table[window + j, 0] = first + j
                    table[window + j, 1] = length[i] - j * WIN
                    table[window + j, 2] = prompt_base
                    table[window + j, 3] = branch_base
                    table[window + j, 4] = prompt // TREE * ELDER
                    table[window + j, 5] = 2 * ELDER + number * 2 * WIN

        return unused

    lax.fori_loop(0, owner.shape[0], visit, 0)


def heads_down(block):
    return jnp.concatenate([block[:, h * HD : (h + 1) * HD] for h in range(HEADS_DEV)], axis=0)


def tile_base(table, w, column, t):
    base = table[w, column] + t * WIN if t < 4 else table[w, column + 1] + (t - 4) * WIN
    return pl.multiple_of(base, WIN)


def for_windows(table, empty, full):
    def window(w, unused):
        count = table[w, 0]
        rows = pl.ds(pl.multiple_of(w * WIN, WIN), WIN)
        for tiles in range(-1, 7):

            @pl.when(count == tiles)
            def _(tiles=tiles):
                if tiles < 0:
                    empty(w, rows)
                else:
                    full(w, rows, tiles)

        return unused

    lax.fori_loop(0, ROWS // WIN, window, 0)


def start_tiles(table, mine_ref, other_ref, pair_buf, sems):
    half = 8 * ELDER

    def window(w, unused):
        for t in range(6):
            base = tile_base(table, w, 2, t)
            there = pair_buf.at[w, pl.ds(t * WIN, WIN), :]

            @pl.when((t < table[w, 0]) & (base < half))
            def _():
                source = mine_ref.at[pl.ds(base, WIN), :]
                pltpu.make_async_copy(source, there, sems.at[w]).start()

            @pl.when((t < table[w, 0]) & (base >= half))
            def _():
                source = other_ref.at[pl.ds(pl.multiple_of(base - half, WIN), WIN), :]
                pltpu.make_async_copy(source, there, sems.at[w]).start()

        return unused

    lax.fori_loop(0, ROWS // WIN, window, 0)


def wait_tiles(w, rows, tiles, mine_ref, own_ref, pair_buf, sems):
    span = tiles * WIN
    if tiles:
        spot = pair_buf.at[w, pl.ds(0, span), :]
        pltpu.make_async_copy(mine_ref.at[pl.ds(0, span), :], spot, sems.at[w]).wait()
    pair_buf[w, span : span + WIN, :] = own_ref[rows, :]
    return pair_buf[w, : span + WIN, :HD], pair_buf[w, : span + WIN, HD:]


def masked(scores, tiles):
    own = scores[tiles * WIN :, :]
    key = lax.broadcasted_iota(jnp.int32, own.shape, 0)
    query = lax.broadcasted_iota(jnp.int32, own.shape, 1) % WIN
    own = jnp.where(key <= query, own, NEG)
    return jnp.concatenate([scores[: tiles * WIN, :], own], axis=0) if tiles else own


def live_columns(table, w):
    place = lax.broadcasted_iota(jnp.int32, (1, HEADS_DEV * WIN), 1) % WIN
    return place < table[w, 1]


def scores_of(query, keys):
    return lax.dot_general(query, keys, (((1,), (1,)), ((), ())), preferred_element_type=F32)


def forward_kernel(
    place, owner, parent, offset, length, query_ref, own_ref, elder_mine_ref,
    elder_other_ref, attn_ref, stat_ref, table, pair_buf, sems,
):
    fill_table(table, place, owner, parent, offset, length)
    start_tiles(table, elder_mine_ref, elder_other_ref, pair_buf, sems)

    def empty(w, rows):
        attn_ref[rows, :] = jnp.zeros((WIN, HEADS_DEV * HD), BF16)

    def full(w, rows, tiles):
        keys, values = wait_tiles(w, rows, tiles, elder_mine_ref, own_ref, pair_buf, sems)
        query = heads_down(query_ref[rows, :])
        scores = masked(scores_of(keys, query), tiles)
        top = jnp.max(scores, axis=0, keepdims=True)
        weights = jnp.exp2((scores - top) * SCALE2)
        total = jnp.sum(weights, axis=0, keepdims=True)
        live = live_columns(table, w)
        attn = lax.dot_general(values, weights.astype(BF16), DOWN, preferred_element_type=F32)
        attn = (attn * jnp.where(live, 1.0 / total, 0.0)).astype(BF16).T
        stat_ref[w, 0:1, :] = jnp.where(live, top * SCALE2 + jnp.log2(total), -NEG)
        for h in range(HEADS_DEV):
            attn_ref[rows, h * HD : (h + 1) * HD] = attn[h * WIN : (h + 1) * WIN]

    for_windows(table, empty, full)


def forward(place, segs, query_rows, own, elders):
    return pl.pallas_call(
        forward_kernel,
        out_shape=(
            jax.ShapeDtypeStruct((ROWS, HEADS_DEV * HD), BF16),
            jax.ShapeDtypeStruct((ROWS // WIN, 8, HEADS_DEV * WIN), F32),
        ),
        in_specs=[SMEM_SPEC] * 5 + [VMEM_SPEC] * 2 + [ANY_SPEC] * 2,
        out_specs=(VMEM_SPEC, VMEM_SPEC),
        scratch_shapes=[
            pltpu.SMEM((6, 8), jnp.int32),
            pltpu.VMEM((6, 7 * WIN, 2 * HD), BF16),
            pltpu.SemaphoreType.DMA((6,)),
        ],
        compiler_params=pltpu.CompilerParams(vmem_limit_bytes=VMEM),
        cost_estimate=pl.CostEstimate(flops=0, bytes_accessed=100_000, transcendentals=0),
        name="attention",
    )(place, *segs, query_rows, own, *elders)


def relative_head(head, k):
    return ((head // 4 + k // 4) % 2) * 4 + (head + k) % 4


def project_kernel(attn_ref, weight_ref, out_ref):
    out_ref[...] = jnp.dot(attn_ref[...], weight_ref[...], preferred_element_type=F32).astype(BF16)


def project(attn, out_weight):
    width = out_weight.shape[1]
    step = 1024
    return pl.pallas_call(
        project_kernel,
        grid=(width // step,),
        out_shape=jax.ShapeDtypeStruct((ROWS, width), BF16),
        in_specs=[
            pl.BlockSpec((ROWS, HEADS_DEV * HD), lambda n: (0, 0)),
            pl.BlockSpec((HEADS_DEV * HD, step), lambda n: (0, n)),
        ],
        out_specs=pl.BlockSpec((ROWS, step), lambda n: (0, n)),
        compiler_params=pltpu.CompilerParams(vmem_limit_bytes=VMEM),
        cost_estimate=pl.CostEstimate(flops=0, bytes_accessed=100_000, transcendentals=0),
        name="project",
    )(attn, out_weight)


def attn_grad_kernel(place, weight_ref, *refs):
    pieces, grad_ref, rows, total = refs[:8], *refs[8:]
    n = pl.program_id(0)
    for k in range(8):
        first = pl.multiple_of(relative_head(place[1], k) * 96, 32)
        rows[pl.ds(first, 96), :] = pieces[k][...]
    part = scores_of(rows[...], weight_ref[...])

    @pl.when(n == 0)
    def _():
        total[...] = part

    @pl.when(n > 0)
    def _():
        total[...] += part

    @pl.when(n == pl.num_programs(0) - 1)
    def _():
        grad_ref[...] = total[...].astype(BF16)


def attn_grad_of(place, out_weight, pieces):
    feats, width = out_weight.shape
    step = 1024
    return pl.pallas_call(
        attn_grad_kernel,
        grid=(width // step,),
        out_shape=jax.ShapeDtypeStruct((ROWS, feats), BF16),
        in_specs=[SMEM_SPEC, pl.BlockSpec((feats, step), lambda n: (0, n))]
        + [pl.BlockSpec((96, step), lambda n: (0, n))] * 8,
        out_specs=pl.BlockSpec((ROWS, feats), lambda n: (0, 0)),
        scratch_shapes=[pltpu.VMEM((ROWS, step), BF16), pltpu.VMEM((ROWS, feats), F32)],
        compiler_params=pltpu.CompilerParams(vmem_limit_bytes=VMEM),
        cost_estimate=pl.CostEstimate(flops=0, bytes_accessed=100_000, transcendentals=0),
        name="attn_grad",
    )(place, out_weight, *pieces)


def weight_grad_kernel(flip, place, attn_ref, *rest):
    pieces, out_ref, turned, rows = rest[:8], *rest[8:]
    leaf = place[0]

    @pl.when(pl.program_id(0) == 0)
    def _():
        turned[...] = attn_ref[...].T

    for core in range(2):

        @pl.when((leaf + flip) % 2 == core)
        def _():
            for k in range(8):
                first = pl.multiple_of(relative_head(place[1], k) * 96, 32)
                for j in range(4):
                    begin = (j * 2 + core) * 256
                    rows[pl.ds(first, 96), j * 256 : (j + 1) * 256] = pieces[k][
                        :, begin : begin + 256
                    ]

    product = jnp.dot(turned[...], rows[...], preferred_element_type=F32).astype(BF16)
    for j in range(4):
        out_ref[j // 2 * 2 + (leaf // 2 + j) % 2] = product[:, j * 256 : (j + 1) * 256]


def weight_grad_of(place, attn, pieces, flip):
    feats, width = HEADS_DEV * HD, pieces[0].shape[1]
    step = width // 2
    return pl.pallas_call(
        functools.partial(weight_grad_kernel, flip),
        grid=(2,),
        in_specs=[SMEM_SPEC, pl.BlockSpec((ROWS, feats), lambda n: (0, 0))]
        + [pl.BlockSpec((96, step), lambda n: (0, n))] * 8,
        out_specs=pl.BlockSpec((4, feats, 256), lambda n: (n, 0, 0)),
        scratch_shapes=[pltpu.VMEM((feats, ROWS), BF16), pltpu.VMEM((ROWS, step // 2), BF16)],
        out_shape=jax.ShapeDtypeStruct((8, feats, 256), BF16),
        compiler_params=pltpu.CompilerParams(vmem_limit_bytes=VMEM),
        cost_estimate=pl.CostEstimate(flops=0, bytes_accessed=100_000, transcendentals=0),
        name="weight_grad",
    )(place, attn, *pieces)


def backward_kernel(
    place, owner, parent, offset, length, query_ref, grad_ref, attn_ref, stat_ref, own_ref,
    elder_mine_ref, elder_other_ref, zero_mine_ref, zero_other_ref, query_grad_ref, own_grad_ref,
    mine_ref, other_ref, table, pair_buf, elder_sum, elder_out, sems, out_sem,
):
    del zero_mine_ref, zero_other_ref
    fill_table(table, place, owner, parent, offset, length)
    start_tiles(table, elder_mine_ref, elder_other_ref, pair_buf, sems)
    elder_sum[...] = jnp.zeros_like(elder_sum)

    def empty(w, rows):
        query_grad_ref[rows, :] = jnp.zeros((WIN, HEADS_DEV * HD), BF16)
        own_grad_ref[rows, :] = jnp.zeros((WIN, 2 * HD), F32)

    def full(w, rows, tiles):
        keys, values = wait_tiles(w, rows, tiles, elder_mine_ref, own_ref, pair_buf, sems)
        query = heads_down(query_ref[rows, :])
        grad = heads_down(grad_ref[rows, :])
        attn = heads_down(attn_ref[rows, :])
        delta = jnp.sum((grad.astype(F32) * attn.astype(F32)).T, axis=0, keepdims=True)
        probs = jnp.exp2(masked(scores_of(keys, query) * SCALE2 - stat_ref[w, 0:1, :], tiles))
        dprobs = scores_of(values, grad)
        dscores = (probs * (dprobs - delta)).astype(BF16)
        query_grad = lax.dot_general(keys, dscores, DOWN, preferred_element_type=F32)
        query_grad = (query_grad * SCALE).astype(BF16).T
        for h in range(HEADS_DEV):
            query_grad_ref[rows, h * HD : (h + 1) * HD] = query_grad[h * WIN : (h + 1) * WIN]
        key_grad = SCALE * jnp.dot(dscores, query, preferred_element_type=F32)
        value_grad = jnp.dot(probs.astype(BF16), grad, preferred_element_type=F32)
        for t in range(tiles):
            spot = pl.ds(tile_base(table, w, 4, t), WIN)
            part = slice(t * WIN, (t + 1) * WIN)
            elder_sum[spot, :HD] += key_grad[part]
            elder_sum[spot, HD:] += value_grad[part]
        own_grad_ref[rows, :HD] = key_grad[tiles * WIN :]
        own_grad_ref[rows, HD:] = value_grad[tiles * WIN :]

    for_windows(table, empty, full)
    elder_out[...] = elder_sum[...].astype(BF16)
    half = 8 * ELDER
    for tree in range(2):
        for level in range(5):
            segment = tree * TREE + level
            count = ELDER if level == 0 else 2 * WIN
            first = tree * ELDER if level == 0 else 2 * ELDER + (tree * 4 + level - 1) * 2 * WIN
            shift = offset[segment] - elder_start(offset[segment])
            base = relative_leaf(place[0], owner[segment]) * ELDER + shift
            source = elder_out.at[pl.ds(first, count), :]

            @pl.when(base < half)
            def _():
                target = mine_ref.at[pl.ds(pl.multiple_of(base, WIN), count), :]
                pltpu.make_async_copy(source, target, out_sem).start()

            @pl.when(base >= half)
            def _():
                target = other_ref.at[pl.ds(pl.multiple_of(base - half, WIN), count), :]
                pltpu.make_async_copy(source, target, out_sem).start()

    pltpu.make_async_copy(elder_out, mine_ref.at[pl.ds(0, SEEN), :], out_sem).wait()


def backward(place, segs, query_rows, grad, attn, stat, own, elders, zeros):
    return pl.pallas_call(
        backward_kernel,
        out_shape=(
            jax.ShapeDtypeStruct((ROWS, HEADS_DEV * HD), BF16),
            jax.ShapeDtypeStruct((ROWS, 2 * HD), F32),
            jax.ShapeDtypeStruct((8 * ELDER, 2 * HD), BF16),
            jax.ShapeDtypeStruct((8 * ELDER, 2 * HD), BF16),
        ),
        in_specs=[SMEM_SPEC] * 5 + [VMEM_SPEC] * 5 + [ANY_SPEC] * 4,
        out_specs=(VMEM_SPEC, VMEM_SPEC, ANY_SPEC, ANY_SPEC),
        input_output_aliases={12: 2, 13: 3},
        scratch_shapes=[
            pltpu.SMEM((6, 8), jnp.int32),
            pltpu.VMEM((6, 7 * WIN, 2 * HD), BF16),
            pltpu.VMEM((SEEN, 2 * HD), F32),
            pltpu.VMEM((SEEN, 2 * HD), BF16),
            pltpu.SemaphoreType.DMA((6,)),
            pltpu.SemaphoreType.DMA,
        ],
        compiler_params=pltpu.CompilerParams(vmem_limit_bytes=VMEM),
        cost_estimate=pl.CostEstimate(flops=0, bytes_accessed=100_000, transcendentals=0),
        name="attention_back",
    )(place, *segs, query_rows, grad, attn, stat, own, *elders, *zeros)


def settle_kernel(place, owner, offset, own_ref, *rest):
    parts, out_ref, total = rest[:2], rest[2], rest[3]
    leaf = place[0]
    total[...] = own_ref[...]

    def find(i, start):
        mine = (owner[i] == leaf) & (i % TREE < 5)
        return jnp.where(mine, elder_start(offset[i]), start)

    start = lax.fori_loop(0, owner.shape[0], find, jnp.int32(0))
    spot = pl.ds(pl.multiple_of(start, WIN), ELDER)
    total[spot, :] += sum(part[...].astype(F32) for part in parts)
    for h in range(8):
        out_ref[h] = total[h * 96 : (h + 1) * 96, :].astype(BF16)


def settle(place, owner, offset, own, parts):
    return pl.pallas_call(
        settle_kernel,
        out_shape=jax.ShapeDtypeStruct((8, 96, 2 * HD), BF16),
        in_specs=[SMEM_SPEC] * 3 + [VMEM_SPEC] * 3,
        out_specs=VMEM_SPEC,
        scratch_shapes=[pltpu.VMEM((ROWS, 2 * HD), F32)],
        compiler_params=pltpu.CompilerParams(vmem_limit_bytes=VMEM),
        cost_estimate=pl.CostEstimate(flops=0, bytes_accessed=100_000, transcendentals=0),
        name="settle",
    )(place, owner, offset, own, *parts)


def exchange(blocks, axis, groups=None):
    return lax.all_to_all(blocks, axis, 0, 0, axis_index_groups=groups)


def spread_depth(blocks):
    depth = lax.axis_index("leaf") // 4
    ahead = [
        lax.dynamic_index_in_dim(blocks, (depth + d) % 4, 0, keepdims=False) for d in range(4)
    ]
    return [ahead[0], *[leaf_perm(ahead[d], d, 0, 0) for d in range(1, 4)]]


def sum_blocks(blocks):
    return add(*[blocks[i] for i in range(blocks.shape[0])])


def shards(
    query_rows, key_rows, value_rows, out_weight, out_grad, seg_owner, seg_parent, seg_offset,
    seg_length,
):
    place = jnp.stack([lax.axis_index("leaf"), lax.axis_index("head")]).astype(jnp.int32)
    segs = (seg_owner, seg_parent, seg_offset, seg_length)
    own, elder = pack(place, seg_owner, seg_offset, key_rows, value_rows)
    pair = jnp.concatenate([elder, leaf_perm(elder, 0, 1, 0)], axis=0)

    before = head_perm(out_grad, 0, 1)
    behind = head_perm(out_grad, 0, -1)
    cross = head_perm(out_grad, 1, 0)
    half = out_grad.shape[0] // 2
    far = jnp.concatenate(
        [head_perm(before[:half], 0, 1), head_perm(behind[half:], 0, -1)], axis=0
    )
    cross_before = head_perm(cross, 0, 1)
    cross_behind = head_perm(cross, 0, -1)
    zeros = empty_elders(after(place, pair))
    elder_mine = jnp.concatenate(
        [pair, *[leaf_perm(pair, -d, 0, 0) for d in range(1, 4)]], axis=0
    )
    elder_mine, far, cross_before, cross_behind, *zeros = lax.optimization_barrier(
        (elder_mine, far, cross_before, cross_behind, *zeros)
    )
    elder_other = leaf_perm(elder_mine, 0, 0, 1)
    cross_far = head_perm(far, 1, 0)
    elders = (elder_mine, elder_other)
    attn, stat = forward(place, segs, query_rows, own, elders)
    partial = project(attn, out_weight)
    partial, cross_far = lax.optimization_barrier((partial, cross_far))

    pieces = [out_grad, behind, far, before, cross, cross_behind, cross_far, cross_before]
    layer_parts = exchange(partial.reshape(8, 96, -1), "head")
    attn_grad = attn_grad_of(place, after(out_weight, partial), pieces)
    query_grads, own_grad, mine_pair, other_pair = backward(
        place, segs, query_rows, attn_grad, attn, stat, own, elders, zeros
    )
    pair_recv = leaf_perm(other_pair, 0, 0, 1)
    other_weight = weight_grad_of(place, after(attn, other_pair), pieces, 1)
    weight_recv = leaf_perm(other_weight, 0, 0, 1)
    pair_joined = add(after(mine_pair, other_weight), pair_recv)
    pair_blocks = pair_joined.reshape(4, 2 * ELDER, 2 * HD)
    pair_parts = [pair_blocks[0], *[leaf_perm(pair_blocks[d], d, 0, 0) for d in range(1, 4)]]
    mine_weight = weight_grad_of(place, after(attn, pair_joined), pieces, 0)
    weight_joined = add(mine_weight, weight_recv)
    weight_joined = after(weight_joined, pair_parts[1])
    weight_parts = spread_depth(weight_joined.reshape(4, 2, *weight_joined.shape[1:]))
    pair_sum = add(*pair_parts)
    pair_sum, layer_parts = lax.optimization_barrier((pair_sum, layer_parts))
    pair_last = leaf_perm(pair_sum[ELDER:], 0, 1, 0)
    layer_out = sum_blocks(layer_parts)
    blocks = settle(place, seg_owner, seg_offset, own_grad, [pair_sum[:ELDER], pair_last])
    weight_parts = [after(part, pair_last) for part in weight_parts]
    weight_sum = add(*weight_parts)
    weight_grad = add(weight_sum[0], leaf_perm(weight_sum[1], 0, 1, 0))
    terms = exchange(blocks, "head")
    first = add(*[terms[h] for h in range(4)])
    second = add(*[terms[h] for h in range(4, 8)])
    key_grads = jnp.concatenate([first[:, :HD], second[:, :HD]], axis=1)
    value_grads = jnp.concatenate([first[:, HD:], second[:, HD:]], axis=1)
    return layer_out, query_grads, key_grads, value_grads, weight_grad


def solution(mesh):
    return jax.shard_map(
        shards,
        mesh=mesh,
        in_specs=(
            P("leaf", "head"),
            P("leaf", None),
            P("leaf", None),
            P("head", None),
            P(("leaf", "head"), None),
            P(),
            P(),
            P(),
            P(),
        ),
        out_specs=(
            P(("leaf", "head"), None),
            P("leaf", "head"),
            P(("leaf", "head"), None),
            P(("leaf", "head"), None),
            P("head", "leaf"),
        ),
        check_vma=False,
    )
```
